512 devices in a mesh: dp: 64 (over y, z), graph: 8 (over x, core).
Axes of the slice: x: 4, y: 8, z: 8, core: 2. Of those that a mesh axis runs over, the one named last changes fastest.
Arguments:
- atoms: bfloat16 [64, 192, 512], P('dp', 'graph'), may hold values from -6 to 6
- cotangent: bfloat16 [64, 192, 512], P('dp', 'graph'), may hold values from -6 to 6
- sources: int32 [64, 4096], P('dp', 'graph'), may hold values from 0 to 191
- targets: int32 [64, 4096], P('dp', 'graph'), may hold values from 0 to 191
- radial: bfloat16 [64, 4096, 128], P('dp', 'graph'), may hold values from 0 to 1
- envelope: float32 [64, 4096], P('dp', 'graph'), may hold values from 0.1 to 1
- edge_counts: int32 [64, 8], P('dp', 'graph'), may hold values from 128 to 512
- source_weight: bfloat16 [512, 1024], replicated, may hold values from -0.25 to 0.25
- radial_weight: bfloat16 [128, 1024], replicated, may hold values from -0.5 to 0.5
- output_weight: bfloat16 [1024, 512], replicated, may hold values from -0.1875 to 0.1875
Outputs:
- updated: bfloat16 [64, 192, 512], P('dp', 'graph')
- grad_atoms: bfloat16 [64, 192, 512], P('dp', 'graph')
- grad_source: bfloat16 [512, 1024], replicated
- grad_output: bfloat16 [1024, 512], replicated
The draws below stay inside these ranges and needn't reach their ends.
All inputs are finite; a program needn't handle non-finite values.
Results may differ from the reference program's by a relative error of at most 0.0057.
Values may be sent and summed in bfloat16 or wider, within the bound.
A program may use at most 64 MiB of HBM per device.

```python
import math
import jax
import jax.numpy as jnp
from jax import lax

DA = 512
DE = 1024
NR = 128
ATOM_DEV = 24
EDGE_DEV = 512
SYSTEMS = 64
ATOMS = 192
EDGES = 4096
N_GRAPH = 8


def touch_ends(entries, key, least, top_value):
    longest = entries.shape.index(max(entries.shape))
    spots = []
    for shift in (0, 1):
        where = [jax.random.randint(jax.random.fold_in(key, axis), (), 0, length) for axis, length in enumerate(entries.shape)]
        where[longest] = (where[longest] + shift) % entries.shape[longest]
        spots.append(tuple(where))
    return entries.at[spots[0]].set(least).at[spots[1]].set(top_value)


def level_of(stream_key, extent, shards, low, top_value):
    def one(position, parts):
        draws = jax.random.uniform(jax.random.fold_in(jax.random.fold_in(stream_key, 6), position), (parts,), jnp.float32, low / len(shards), top_value / len(shards))
        return jnp.repeat(jnp.exp(draws), extent[position] // parts).reshape((-1,) + (1,) * (len(extent) - position - 1))

    factor_of = one(*shards[0])
    for cut in shards[1:]:
        factor_of = factor_of * one(*cut)
    return factor_of


def centred(own_key, dims, spread, reach, shards=(), held_as=jnp.bfloat16):
    array = jax.random.normal(own_key, dims, jnp.float32) * spread
    if len(shards) > 0:
        array = level_of(own_key, dims, shards, -0.22, 0.18) * array
    return jnp.clip(array, min=-reach, max=reach).astype(held_as)


def setup_inputs(seed: int = 0) -> dict:
    key_list = jax.random.split(jax.random.key(seed), 11)
    return {
        "atoms": centred(key_list[0], (SYSTEMS, ATOMS, DA), 1.0, 6.0, ((0, 64), (1, 8))),
        "cotangent": centred(key_list[1], (SYSTEMS, ATOMS, DA), 1.0, 6.0, ((0, 64), (1, 8))),
        "sources": touch_ends(jax.random.randint(key_list[2], (SYSTEMS, EDGES), 0, ATOMS), jax.random.fold_in(key_list[2], 1), 0, ATOMS - 1).astype(jnp.int32),
        "targets": touch_ends(jax.random.randint(key_list[3], (SYSTEMS, EDGES), 0, ATOMS), jax.random.fold_in(key_list[3], 1), 0, ATOMS - 1).astype(jnp.int32),
        "radial": jnp.clip(1.0 * jax.random.uniform(key_list[4], (SYSTEMS, EDGES, NR), jnp.float32) ** level_of(key_list[4], (SYSTEMS, EDGES, NR), ((0, 64), (1, 8)), -0.2, 0.2), 0.0, 1.0).astype(jnp.bfloat16),
        "envelope": jnp.clip(0.1 + 0.9 * jax.random.uniform(key_list[5], (SYSTEMS, EDGES), jnp.float32) ** level_of(key_list[5], (SYSTEMS, EDGES), ((0, 64), (1, 8)), -0.2, 0.2), 0.1, 1.0),
        "edge_counts": touch_ends(jax.random.randint(key_list[6], (SYSTEMS, N_GRAPH), EDGE_DEV // 4, EDGE_DEV + 1), jax.random.fold_in(key_list[6], 1), EDGE_DEV // 4, EDGE_DEV).astype(jnp.int32),
        "source_weight": centred(key_list[7], (DA, DE), DA ** -0.5, 0.25),
        "radial_weight": centred(key_list[8], (NR, DE), NR ** -0.5, 0.5),
        "output_weight": centred(key_list[9], (DE, DA), DE ** -0.5, 0.1875),
    }


def reference(atoms, cotangent, sources, targets, radial, envelope, edge_counts, source_weight, radial_weight, output_weight):
    scale = math.sqrt(ATOM_DEV / EDGE_DEV)
    positions = jnp.arange(EDGES, dtype=jnp.int32)
    slots = positions % EDGE_DEV
    owners = positions // EDGE_DEV

    def system(carry, inputs):
        acc_source, acc_output = carry
        embed, adjoint, src_ids, dst_ids, basis, decay, counts = inputs
        gathered = embed[src_ids]
        pre = jnp.dot(basis, radial_weight, preferred_element_type=jnp.float32) + jnp.dot(gathered, source_weight, preferred_element_type=jnp.float32)
        live = (slots < counts[owners]).astype(jnp.float32)
        weight = decay * live
        sigma = jax.nn.sigmoid(pre)
        message = (pre * sigma * weight[:, None]).astype(jnp.bfloat16)
        summed = jax.ops.segment_sum(message.astype(jnp.float32), dst_ids, num_segments=ATOMS).astype(jnp.bfloat16)
        update = jnp.dot(summed, output_weight, preferred_element_type=jnp.float32) * scale
        result = (embed.astype(jnp.float32) + update).astype(jnp.bfloat16)
        back = (jnp.dot(adjoint, output_weight.T, preferred_element_type=jnp.float32) * scale).astype(jnp.bfloat16)
        pulled = back[dst_ids]
        slope = sigma * (1.0 + pre * (1.0 - sigma))
        dpre = (pulled.astype(jnp.float32) * weight[:, None] * slope).astype(jnp.bfloat16)
        acc_source = acc_source + jnp.dot(gathered.T, dpre, preferred_element_type=jnp.float32)
        acc_output = acc_output + jnp.dot(summed.T, adjoint, preferred_element_type=jnp.float32) * scale
        dgathered = jnp.dot(dpre, source_weight.T, preferred_element_type=jnp.float32).astype(jnp.bfloat16)
        pushed = jax.ops.segment_sum(dgathered.astype(jnp.float32), src_ids, num_segments=ATOMS)
        grad = (adjoint.astype(jnp.float32) + pushed).astype(jnp.bfloat16)
        return ((acc_source, acc_output), (result, grad))
    start = (jnp.zeros((DA, DE), jnp.float32), jnp.zeros((DE, DA), jnp.float32))
    (acc_source, acc_output), (updated, grad_atoms) = lax.scan(system, start, (atoms, cotangent, sources, targets, radial, envelope, edge_counts))
    grad_source = (acc_source * (16.0 / math.sqrt(SYSTEMS * EDGES))).astype(jnp.bfloat16)
    grad_output = (acc_output * (1.0 / math.sqrt(SYSTEMS * ATOMS))).astype(jnp.bfloat16)
    return (updated, grad_atoms, grad_source, grad_output)
```

```python
import functools
import math

import jax
import jax.numpy as jnp
from jax import lax
from jax.experimental import pallas as pl
from jax.experimental.pallas import tpu as pltpu
from jax.sharding import PartitionSpec as P

MESH = pl.DeviceIdType.MESH
F32 = jnp.float32
BF16 = jnp.bfloat16

OWN = 24
SLOT = 2 * OWN
ATOMS = 192
EDGES = 512
DA = 512
DE = 1024
PAD = 32
COLS = 128
SIDE = 8


def dot(left, right):
    return jnp.dot(left, right, preferred_element_type=F32)


def dot_nt(left, right):
    return lax.dot_general(left, right, (((1,), (1,)), ((), ())), preferred_element_type=F32)


def dot_tn(left, right):
    return lax.dot_general(left, right, (((0,), (0,)), ((), ())), preferred_element_type=F32)


def body(
    atoms_ref,
    cot_ref,
    src_ref,
    dst_ref,
    radial_ref,
    env_ref,
    count_ref,
    sw_ref,
    rw_ref,
    ow_ref,
    updated_ref,
    grad_atoms_ref,
    out1,
    out2,
    full,
    atoms_s,
    back_s,
    gathered_s,
    hot_dst_s,
    hott_src_s,
    hott_dst_s,
    cols_s,
    msg_s,
    dpre_s,
    stage,
    recv,
    rows_out,
    rows_in,
    ga,
    gb,
    ra,
    rb,
    sa,
    sb,
    qa,
    qb,
    fa,
    fb,
    full_send,
    full_recv,
    rs_send,
    rs_recv,
    row_send,
    row_recv,
    r1_send,
    r1_recv,
    r2_send,
    r2_recv,
    r3_send,
    r3_recv,
    r4_send,
    r4_recv,
    x_send,
    x_recv,
    c_send,
    c_recv,
):
    dp = lax.axis_index("dp")
    g = lax.axis_index("graph")
    y, z = lax.div(dp, SIDE), lax.rem(dp, SIDE)
    x, core = lax.div(g, 2), lax.rem(g, 2)
    other = 1 - core
    scale = math.sqrt(OWN / EDGES)
    sends = []

    def copy(src, dst, send, recv_sem, device):
        c = pltpu.make_async_remote_copy(
            src_ref=src, dst_ref=dst, send_sem=send, recv_sem=recv_sem, device_id=device, device_id_type=MESH
        )
        c.start()
        sends.append(c)

    def arrived(dst, recv_sem):
        pltpu.make_async_remote_copy(
            src_ref=dst, dst_ref=dst, send_sem=recv_sem, recv_sem=recv_sem, device_id=(dp, g), device_id_type=MESH
        ).wait_recv()

    graph_peers = [(dp, lax.rem(g + k, 8)) for k in range(1, 8)]
    y_at = [lax.rem(y + k, SIDE) for k in range(SIDE)]
    z_at = [lax.rem(z + k, SIDE) for k in range(SIDE)]
    y_peers = [(y_at[k] * SIDE + z, g) for k in range(SIDE)]
    z_peers = [(y * SIDE + z_at[k], g) for k in range(SIDE)]

    barrier = pltpu.get_barrier_semaphore()
    for peer in graph_peers + y_peers[1:] + z_peers[1:]:
        pl.semaphore_signal(barrier, inc=1, device_id=peer, device_id_type=MESH)

    full[g] = jnp.concatenate([atoms_ref[0], cot_ref[0]], axis=0)
    pl.semaphore_wait(barrier, 21)
    for k in range(1, 8):
        copy(full.at[g], full.at[g], full_send.at[k], full_recv.at[g], graph_peers[k - 1])

    src_row = src_ref[...]
    dst_row = dst_ref[...]
    slots = lax.broadcasted_iota(jnp.int32, (1, EDGES), 1)
    live = (slots < count_ref[0, 0]).astype(F32)
    weight_row = env_ref[...] * live
    table = jnp.concatenate(
        [src_row.astype(F32), dst_row.astype(F32), weight_row, jnp.zeros((5, EDGES), F32)], axis=0
    )
    cols_s[...] = table.T
    atom_rows = lax.broadcasted_iota(jnp.int32, (ATOMS, EDGES), 0)
    hott_src_s[...] = (atom_rows == src_row).astype(F32).astype(BF16)
    hott_dst_s[...] = (atom_rows == dst_row).astype(F32).astype(BF16)
    atom_cols = lax.broadcasted_iota(jnp.int32, (EDGES, ATOMS), 1).astype(F32)
    hot_src = (atom_cols == cols_s[:, 0:1]).astype(F32).astype(BF16)
    hot_dst_s[...] = (atom_cols == cols_s[:, 1:2]).astype(F32).astype(BF16)
    pick_r = lax.broadcasted_iota(jnp.int32, (ATOMS, 8 * SLOT), 0)
    pick_c = lax.broadcasted_iota(jnp.int32, (ATOMS, 8 * SLOT), 1)
    pick_at = pick_r + OWN * ((pick_r * 683) >> 14)
    pick_atoms = (pick_c == pick_at).astype(F32).astype(BF16)
    pick_cot = (pick_c == pick_at + OWN).astype(F32).astype(BF16)

    for k in range(1, 8):
        peer = lax.rem(g + k, 8)
        arrived(full.at[peer], full_recv.at[peer])
    both = full[...].reshape(8 * SLOT, DA)
    atoms = dot(pick_atoms, both).astype(BF16)
    cot = dot(pick_cot, both).astype(BF16)
    atoms_s[0] = atoms
    atoms_s[1] = cot
    gathered_s[...] = dot(hot_src, atoms).astype(BF16)
    back_s[...] = (dot_nt(cot, ow_ref[...]) * scale).astype(BF16)

    for dx in (2, 1, 3, 0):
        xt = lax.rem(x + dx, 4)
        cols = pl.ds(pl.multiple_of(xt * 2 * COLS, 2 * COLS), 2 * COLS)
        for r in range(4):
            rows = slice(r * 128, (r + 1) * 128)
            pre = dot(radial_ref[0, rows, :], rw_ref[:, cols]) + dot(gathered_s[rows, :], sw_ref[:, cols])
            pulled = dot(hot_dst_s[rows, :], back_s[:, cols])
            weight = cols_s[rows, 2:3]
            sigma = jax.nn.sigmoid(pre)
            msg_s[rows, :] = (pre * sigma * weight).astype(BF16)
            slope = sigma * (1.0 + pre * (1.0 - sigma))
            dpre_s[rows, :] = (pulled * weight * slope).astype(BF16)
        part = dot(hott_dst_s[...], msg_s[...]).astype(BF16)
        stage[dx, 0, 0] = part[:, :COLS]
        stage[dx, 1, 0] = part[:, COLS:]
        part = dot(hott_src_s[...], dpre_s[...]).astype(BF16)
        stage[dx, 0, 1] = part[:, :COLS]
        stage[dx, 1, 1] = part[:, COLS:]
        if dx:
            for cc in range(2):
                copy(
                    stage.at[dx, cc],
                    recv.at[2 * dx + core],
                    rs_send.at[2 * dx + cc],
                    rs_recv.at[2 * dx + core],
                    (dp, 2 * xt + cc),
                )
        else:
            copy(stage.at[0, other], recv.at[core], rs_send.at[0], rs_recv.at[core], (dp, 2 * x + other))

    total = stage[0, core].astype(F32)
    for slot in (other, 4, 5, 2, 3, 6, 7):
        arrived(recv.at[slot], rs_recv.at[slot])
        total = total + recv[slot].astype(F32)
    sums = total.astype(BF16)
    summed, dsum = sums[0], sums[1]

    grow_r = lax.broadcasted_iota(jnp.int32, (8 * PAD, ATOMS), 0)
    grow_c = lax.broadcasted_iota(jnp.int32, (8 * PAD, ATOMS), 1)
    inner = grow_r & (PAD - 1)
    grow = ((inner < OWN) & (grow_c == (grow_r >> 5) * OWN + inner)).astype(F32).astype(BF16)
    rows_out[:, 0] = dot(grow, summed).astype(BF16).reshape(8, PAD, COLS)
    rows_out[:, 1] = dot(grow, dsum).astype(BF16).reshape(8, PAD, COLS)
    own_cols = pl.ds(pl.multiple_of(g * COLS, COLS), COLS)
    rows_in[:, :, own_cols] = rows_out[g]

    ga[...] = dot_tn(summed, atoms_s[1]).astype(BF16).reshape(SIDE, 16, DA)
    gb[...] = dot_tn(atoms_s[0], dsum).astype(BF16).reshape(SIDE, 64, COLS)
    for k in range(1, SIDE):
        copy(ga.at[y_at[k]], ra.at[k], r1_send.at[0, k], r1_recv.at[0, k], y_peers[k])
        copy(gb.at[z_at[k]], rb.at[k], r1_send.at[1, k], r1_recv.at[1, k], z_peers[k])
    for k in range(1, 8):
        peer = lax.rem(g + k, 8)
        copy(rows_out.at[peer], rows_in.at[:, :, own_cols], row_send.at[k], row_recv.at[g], (dp, peer))

    sum_a = ga[y].astype(F32)
    sum_b = gb[z].astype(F32)
    for k in range(1, SIDE):
        arrived(ra.at[k], r1_recv.at[0, k])
        sum_a = sum_a + ra[k].astype(F32)
        arrived(rb.at[k], r1_recv.at[1, k])
        sum_b = sum_b + rb[k].astype(F32)
    for j in range(SIDE):
        sa[j] = sum_a[8 * (j // 4) : 8 * (j // 4) + 8, 128 * (j % 4) : 128 * (j % 4) + 128]
    sb[...] = sum_b.reshape(SIDE, 8, COLS)
    for k in range(1, SIDE):
        copy(sa.at[z_at[k]], qa.at[k], r2_send.at[0, k], r2_recv.at[0, k], z_peers[k])
        copy(sb.at[y_at[k]], qb.at[k], r2_send.at[1, k], r2_recv.at[1, k], y_peers[k])

    sum_a = sa[z]
    sum_b = sb[y]
    for k in range(1, SIDE):
        arrived(qa.at[k], r2_recv.at[0, k])
        sum_a = sum_a + qa[k]
        arrived(qb.at[k], r2_recv.at[1, k])
        sum_b = sum_b + qb[k]
    systems = SIDE * SIDE
    fa[z] = sum_a * (scale / math.sqrt(systems * ATOMS))
    fb[y] = sum_b * (16.0 / math.sqrt(systems * 8 * EDGES))
    for k in range(1, SIDE):
        copy(fa.at[z], fa.at[z], r3_send.at[0, k], r3_recv.at[0, z], z_peers[k])
        copy(fb.at[y], fb.at[y], r3_send.at[1, k], r3_recv.at[1, y], y_peers[k])

    for k in range(1, 8):
        peer = lax.rem(g + k, 8)
        peer_cols = pl.ds(pl.multiple_of(peer * COLS, COLS), COLS)
        arrived(rows_in.at[:, :, peer_cols], row_recv.at[peer])
    update = dot(rows_in[0], ow_ref[...]) * scale
    updated_ref[0] = (atoms_ref[0].astype(F32) + update[:OWN]).astype(BF16)
    pushed = dot_nt(rows_in[1], sw_ref[...])
    grad_atoms_ref[0] = (cot_ref[0].astype(F32) + pushed[:OWN]).astype(BF16)

    for k in range(1, SIDE):
        arrived(fa.at[z_at[k]], r3_recv.at[0, z_at[k]])
        arrived(fb.at[y_at[k]], r3_recv.at[1, y_at[k]])
    halves = [jnp.concatenate([fa[4 * h + j] for j in range(4)], axis=1) for h in range(2)]
    out1[g, y] = jnp.concatenate(halves, axis=0).astype(BF16)
    out2[g, z] = fb[...].reshape(64, COLS).astype(BF16)
    for k in range(1, SIDE):
        copy(out1.at[g, y], out1.at[g, y], r4_send.at[0, k], r4_recv.at[0, y], y_peers[k])
        copy(out2.at[g, z], out2.at[g, z], r4_send.at[1, k], r4_recv.at[1, z], z_peers[k])
    for k in range(1, SIDE):
        arrived(out1.at[g, y_at[k]], r4_recv.at[0, y_at[k]])
        arrived(out2.at[g, z_at[k]], r4_recv.at[1, z_at[k]])

    right, left, far = (lax.rem(x + k, 4) for k in (1, 3, 2))
    to_right, to_left, to_other = (dp, 2 * right + core), (dp, 2 * left + core), (dp, 2 * x + other)
    g_right, g_left, g_far = 2 * right + core, 2 * left + core, 2 * far + core

    def pass_on(out, sem, block, slot, device):
        copy(out.at[block], out.at[block], x_send.at[sem, slot], x_recv.at[sem, slot], device)

    def swap(out, sem, block, slot):
        copy(out.at[block], out.at[block], c_send.at[sem, slot], c_recv.at[sem, slot], to_other)

    pass_on(out1, 0, g, 0, to_right)
    pass_on(out2, 1, g, 1, to_left)
    pass_on(out1, 0, g, 1, to_left)
    pass_on(out2, 1, g, 0, to_right)
    swap(out1, 0, g, 0)
    swap(out2, 1, g, 0)
    arrived(out1.at[g_left], x_recv.at[0, 0])
    pass_on(out1, 0, g_left, 2, to_right)
    arrived(out2.at[g_right], x_recv.at[1, 1])
    pass_on(out2, 1, g_right, 2, to_left)
    swap(out1, 0, g_left, 1)
    swap(out2, 1, g_right, 2)
    arrived(out1.at[g_right], x_recv.at[0, 1])
    swap(out1, 0, g_right, 2)
    arrived(out2.at[g_left], x_recv.at[1, 0])
    swap(out2, 1, g_left, 1)
    arrived(out1.at[g_far], x_recv.at[0, 2])
    swap(out1, 0, g_far, 3)
    arrived(out2.at[g_far], x_recv.at[1, 2])
    swap(out2, 1, g_far, 3)
    for slot, block in enumerate((x, left, right, far)):
        arrived(out1.at[2 * block + other], c_recv.at[0, slot])
        arrived(out2.at[2 * block + other], c_recv.at[1, slot])
    for c in sends:
        c.wait_send()


def local(*args):
    vmem = pl.BlockSpec(memory_space=pltpu.VMEM)
    smem = pl.BlockSpec(memory_space=pltpu.SMEM)
    dma = pltpu.SemaphoreType.DMA
    updated, grad_atoms, out1, out2 = pl.pallas_call(
        body,
        out_shape=(
            jax.ShapeDtypeStruct((1, OWN, DA), BF16),
            jax.ShapeDtypeStruct((1, OWN, DA), BF16),
            jax.ShapeDtypeStruct((8, SIDE, 16, DA), BF16),
            jax.ShapeDtypeStruct((8, SIDE, 64, COLS), BF16),
        ),
        in_specs=[vmem] * 6 + [smem] + [vmem] * 3,
        out_specs=(vmem,) * 4,
        scratch_shapes=[
            pltpu.VMEM((8, SLOT, DA), BF16),
            pltpu.VMEM((2, ATOMS, DA), BF16),
            pltpu.VMEM((ATOMS, DE), BF16),
            pltpu.VMEM((EDGES, DA), BF16),
            pltpu.VMEM((EDGES, ATOMS), BF16),
            pltpu.VMEM((ATOMS, EDGES), BF16),
            pltpu.VMEM((ATOMS, EDGES), BF16),
            pltpu.VMEM((EDGES, 8), F32),
            pltpu.VMEM((EDGES, 2 * COLS), BF16),
            pltpu.VMEM((EDGES, 2 * COLS), BF16),
            pltpu.VMEM((4, 2, 2, ATOMS, COLS), BF16),
            pltpu.VMEM((8, 2, ATOMS, COLS), BF16),
            pltpu.VMEM((8, 2, PAD, COLS), BF16),
            pltpu.VMEM((2, PAD, DE), BF16),
            pltpu.VMEM((SIDE, 16, DA), BF16),
            pltpu.VMEM((SIDE, 64, COLS), BF16),
            pltpu.VMEM((SIDE, 16, DA), BF16),
            pltpu.VMEM((SIDE, 64, COLS), BF16),
            pltpu.VMEM((SIDE, 8, COLS), F32),
            pltpu.VMEM((SIDE, 8, COLS), F32),
            pltpu.VMEM((SIDE, 8, COLS), F32),
            pltpu.VMEM((SIDE, 8, COLS), F32),
            pltpu.VMEM((SIDE, 8, COLS), F32),
            pltpu.VMEM((SIDE, 8, COLS), F32),
            dma((8,)),
            dma((8,)),
            dma((8,)),
            dma((8,)),
            dma((8,)),
            dma((8,)),
            dma((2, SIDE)),
            dma((2, SIDE)),
            dma((2, SIDE)),
            dma((2, SIDE)),
            dma((2, SIDE)),
            dma((2, SIDE)),
            dma((2, SIDE)),
            dma((2, SIDE)),
            dma((2, 3)),
            dma((2, 3)),
            dma((2, 4)),
            dma((2, 4)),
        ],
        compiler_params=pltpu.CompilerParams(
            collective_id=0, has_side_effects=True, vmem_limit_bytes=48 * 1024 * 1024
        ),
    )(*args)
    grad_output = out1.reshape(DE, DA)
    grad_source = out2.reshape(8, DA, COLS).transpose(1, 0, 2).reshape(DA, DE)
    return updated, grad_atoms, grad_source, grad_output


def solution(mesh):
    rows = P("dp", "graph", None)
    flat = P("dp", "graph")
    return jax.shard_map(
        local,
        mesh=mesh,
        in_specs=(rows, rows, flat, flat, rows, flat, flat, P(), P(), P()),
        out_specs=(rows, rows, P(), P()),
        check_vma=False,
    )
```

```python
import functools
import math

import jax
import jax.numpy as jnp
from jax import lax
from jax.experimental import pallas as pl
from jax.experimental.pallas import tpu as pltpu
from jax.sharding import PartitionSpec as P

MESH = pl.DeviceIdType.MESH
F32 = jnp.float32
BF16 = jnp.bfloat16

OWN = 24
SLOT = 2 * OWN
ATOMS = 192
EDGES = 512
DA = 512
DE = 1024
PAD = 32
COLS = 128
SIDE = 8


def dot(left, right):
    return jnp.dot(left, right, preferred_element_type=F32)


def dot_nt(left, right):
    return lax.dot_general(left, right, (((1,), (1,)), ((), ())), preferred_element_type=F32)


def dot_tn(left, right):
    return lax.dot_general(left, right, (((0,), (0,)), ((), ())), preferred_element_type=F32)


def body(
    count_ref,
    *refs,
):
    inputs, refs = refs[:9], refs[9:]
    updated_ref, grad_atoms_ref, out1, out2 = refs[:4]
    held = refs[4:13]
    atoms_ref, cot_ref, src_ref, dst_ref, radial_ref, env_ref, sw_ref, rw_ref, ow_ref = held
    (
        full,
        atoms_s,
        back_s,
        gathered_s,
        hot_dst_s,
        hott_src_s,
        hott_dst_s,
        cols_s,
        msg_s,
        dpre_s,
        stage,
        recv,
        rows_out,
        rows_in,
        ga,
        gb,
        ra,
        rb,
        sa,
        sb,
        qa,
        qb,
        fa,
        fb,
        full_send,
        full_recv,
        rs_send,
        rs_recv,
        row_send,
        row_recv,
        r1_send,
        r1_recv,
        r2_send,
        r2_recv,
        r3_send,
        r3_recv,
        r4_send,
        r4_recv,
        x_send,
        x_recv,
        c_send,
        c_recv,
        load_sem,
    ) = refs[13:]
    dp = lax.axis_index("dp")
    g = lax.axis_index("graph")
    y, z = lax.div(dp, SIDE), lax.rem(dp, SIDE)
    x, core = lax.div(g, 2), lax.rem(g, 2)
    other = 1 - core
    scale = math.sqrt(OWN / EDGES)
    sends = []
    loads = [pltpu.make_async_copy(a, b, load_sem.at[i]) for i, (a, b) in enumerate(zip(inputs, held))]
    for load in loads:
        load.start()

    def copy(src, dst, send, recv_sem, device):
        c = pltpu.make_async_remote_copy(
            src_ref=src, dst_ref=dst, send_sem=send, recv_sem=recv_sem, device_id=device, device_id_type=MESH
        )
        c.start()
        sends.append(c)

    def arrived(dst, recv_sem):
        pltpu.make_async_remote_copy(
            src_ref=dst, dst_ref=dst, send_sem=recv_sem, recv_sem=recv_sem, device_id=(dp, g), device_id_type=MESH
        ).wait_recv()

    graph_peers = [(dp, lax.rem(g + k, 8)) for k in range(1, 8)]
    y_at = [lax.rem(y + k, SIDE) for k in range(SIDE)]
    z_at = [lax.rem(z + k, SIDE) for k in range(SIDE)]
    y_peers = [(y_at[k] * SIDE + z, g) for k in range(SIDE)]
    z_peers = [(y * SIDE + z_at[k], g) for k in range(SIDE)]

    barrier = pltpu.get_barrier_semaphore()
    for peer in graph_peers + y_peers[1:] + z_peers[1:]:
        pl.semaphore_signal(barrier, inc=1, device_id=peer, device_id_type=MESH)

    loads[0].wait()
    loads[1].wait()
    full[g] = jnp.concatenate([atoms_ref[0], cot_ref[0]], axis=0)
    pl.semaphore_wait(barrier, 21)
    for k in range(1, 8):
        copy(full.at[g], full.at[g], full_send.at[k], full_recv.at[g], graph_peers[k - 1])

    for i in (2, 3, 5):
        loads[i].wait()
    src_row = src_ref[...]
    dst_row = dst_ref[...]
    slots = lax.broadcasted_iota(jnp.int32, (1, EDGES), 1)
    live = (slots < count_ref[0, 0]).astype(F32)
    weight_row = env_ref[...] * live
    table = jnp.concatenate(
        [src_row.astype(F32), dst_row.astype(F32), weight_row, jnp.zeros((5, EDGES), F32)], axis=0
    )
    cols_s[...] = table.T
    atom_rows = lax.broadcasted_iota(jnp.int32, (ATOMS, EDGES), 0)
    hott_src_s[...] = (atom_rows == src_row).astype(F32).astype(BF16)
    hott_dst_s[...] = (atom_rows == dst_row).astype(F32).astype(BF16)
    atom_cols = lax.broadcasted_iota(jnp.int32, (EDGES, ATOMS), 1).astype(F32)
    hot_src = (atom_cols == cols_s[:, 0:1]).astype(F32).astype(BF16)
    hot_dst_s[...] = (atom_cols == cols_s[:, 1:2]).astype(F32).astype(BF16)
    pick_r = lax.broadcasted_iota(jnp.int32, (ATOMS, 8 * SLOT), 0)
    pick_c = lax.broadcasted_iota(jnp.int32, (ATOMS, 8 * SLOT), 1)
    pick_at = pick_r + OWN * ((pick_r * 683) >> 14)
    pick_atoms = (pick_c == pick_at).astype(F32).astype(BF16)
    pick_cot = (pick_c == pick_at + OWN).astype(F32).astype(BF16)

    for k in range(1, 8):
        peer = lax.rem(g + k, 8)
        arrived(full.at[peer], full_recv.at[peer])
    for i in (4, 6, 7, 8):
        loads[i].wait()
    both = full[...].reshape(8 * SLOT, DA)
    atoms = dot(pick_atoms, both).astype(BF16)
    cot = dot(pick_cot, both).astype(BF16)
    atoms_s[0] = atoms
    atoms_s[1] = cot
    gathered_s[...] = dot(hot_src, atoms).astype(BF16)
    back_s[...] = (dot_nt(cot, ow_ref[...]) * scale).astype(BF16)

    for dx in (2, 1, 3, 0):
        xt = lax.rem(x + dx, 4)
        cols = pl.ds(pl.multiple_of(xt * 2 * COLS, 2 * COLS), 2 * COLS)
        for r in range(4):
            rows = slice(r * 128, (r + 1) * 128)
            pre = dot(radial_ref[0, rows, :], rw_ref[:, cols]) + dot(gathered_s[rows, :], sw_ref[:, cols])
            pulled = dot(hot_dst_s[rows, :], back_s[:, cols])
            weight = cols_s[rows, 2:3]
            sigma = jax.nn.sigmoid(pre)
            msg_s[rows, :] = (pre * sigma * weight).astype(BF16)
            slope = sigma * (1.0 + pre * (1.0 - sigma))
            dpre_s[rows, :] = (pulled * weight * slope).astype(BF16)
        part = dot(hott_dst_s[...], msg_s[...]).astype(BF16)
        stage[dx, 0, 0] = part[:, :COLS]
        stage[dx, 1, 0] = part[:, COLS:]
        part = dot(hott_src_s[...], dpre_s[...]).astype(BF16)
        stage[dx, 0, 1] = part[:, :COLS]
        stage[dx, 1, 1] = part[:, COLS:]
        if dx:
            for cc in range(2):
                copy(
                    stage.at[dx, cc],
                    recv.at[2 * dx + core],
                    rs_send.at[2 * dx + cc],
                    rs_recv.at[2 * dx + core],
                    (dp, 2 * xt + cc),
                )
        else:
            copy(stage.at[0, other], recv.at[core], rs_send.at[0], rs_recv.at[core], (dp, 2 * x + other))

    total = stage[0, core].astype(F32)
    for slot in (other, 4, 5, 2, 3, 6, 7):
        arrived(recv.at[slot], rs_recv.at[slot])
        total = total + recv[slot].astype(F32)
    sums = total.astype(BF16)
    summed, dsum = sums[0], sums[1]

    grow_r = lax.broadcasted_iota(jnp.int32, (8 * PAD, ATOMS), 0)
    grow_c = lax.broadcasted_iota(jnp.int32, (8 * PAD, ATOMS), 1)
    inner = grow_r & (PAD - 1)
    grow = ((inner < OWN) & (grow_c == (grow_r >> 5) * OWN + inner)).astype(F32).astype(BF16)
    rows_out[:, 0] = dot(grow, summed).astype(BF16).reshape(8, PAD, COLS)
    rows_out[:, 1] = dot(grow, dsum).astype(BF16).reshape(8, PAD, COLS)
    own_cols = pl.ds(pl.multiple_of(g * COLS, COLS), COLS)
    rows_in[:, :, own_cols] = rows_out[g]

    ga[...] = dot_tn(summed, atoms_s[1]).astype(BF16).reshape(SIDE, 16, DA)
    gb[...] = dot_tn(atoms_s[0], dsum).astype(BF16).reshape(SIDE, 64, COLS)
    for k in range(1, SIDE):
        copy(ga.at[y_at[k]], ra.at[k], r1_send.at[0, k], r1_recv.at[0, k], y_peers[k])
        copy(gb.at[z_at[k]], rb.at[k], r1_send.at[1, k], r1_recv.at[1, k], z_peers[k])
    for k in range(1, 8):
        peer = lax.rem(g + k, 8)
        copy(rows_out.at[peer], rows_in.at[:, :, own_cols], row_send.at[k], row_recv.at[g], (dp, peer))

    sum_a = ga[y].astype(F32)
    sum_b = gb[z].astype(F32)
    for k in range(1, SIDE):
        arrived(ra.at[k], r1_recv.at[0, k])
        sum_a = sum_a + ra[k].astype(F32)
        arrived(rb.at[k], r1_recv.at[1, k])
        sum_b = sum_b + rb[k].astype(F32)
    for j in range(SIDE):
        sa[j] = sum_a[8 * (j // 4) : 8 * (j // 4) + 8, 128 * (j % 4) : 128 * (j % 4) + 128]
    sb[...] = sum_b.reshape(SIDE, 8, COLS)
    for k in range(1, SIDE):
        copy(sa.at[z_at[k]], qa.at[k], r2_send.at[0, k], r2_recv.at[0, k], z_peers[k])
        copy(sb.at[y_at[k]], qb.at[k], r2_send.at[1, k], r2_recv.at[1, k], y_peers[k])

    sum_a = sa[z]
    sum_b = sb[y]
    for k in range(1, SIDE):
        arrived(qa.at[k], r2_recv.at[0, k])
        sum_a = sum_a + qa[k]
        arrived(qb.at[k], r2_recv.at[1, k])
        sum_b = sum_b + qb[k]
    systems = SIDE * SIDE
    fa[z] = sum_a * (scale / math.sqrt(systems * ATOMS))
    fb[y] = sum_b * (16.0 / math.sqrt(systems * 8 * EDGES))
    for k in range(1, SIDE):
        copy(fa.at[z], fa.at[z], r3_send.at[0, k], r3_recv.at[0, z], z_peers[k])
        copy(fb.at[y], fb.at[y], r3_send.at[1, k], r3_recv.at[1, y], y_peers[k])

    for k in range(1, 8):
        peer = lax.rem(g + k, 8)
        peer_cols = pl.ds(pl.multiple_of(peer * COLS, COLS), COLS)
        arrived(rows_in.at[:, :, peer_cols], row_recv.at[peer])
    update = dot(rows_in[0], ow_ref[...]) * scale
    updated_ref[0] = (atoms_ref[0].astype(F32) + update[:OWN]).astype(BF16)
    pushed = dot_nt(rows_in[1], sw_ref[...])
    grad_atoms_ref[0] = (cot_ref[0].astype(F32) + pushed[:OWN]).astype(BF16)

    for k in range(1, SIDE):
        arrived(fa.at[z_at[k]], r3_recv.at[0, z_at[k]])
        arrived(fb.at[y_at[k]], r3_recv.at[1, y_at[k]])
    halves = [jnp.concatenate([fa[4 * h + j] for j in range(4)], axis=1) for h in range(2)]
    out1[g, y] = jnp.concatenate(halves, axis=0).astype(BF16)
    out2[g, z] = fb[...].reshape(64, COLS).astype(BF16)
    for k in range(1, SIDE):
        copy(out1.at[g, y], out1.at[g, y], r4_send.at[0, k], r4_recv.at[0, y], y_peers[k])
        copy(out2.at[g, z], out2.at[g, z], r4_send.at[1, k], r4_recv.at[1, z], z_peers[k])
    for k in range(1, SIDE):
        arrived(out1.at[g, y_at[k]], r4_recv.at[0, y_at[k]])
        arrived(out2.at[g, z_at[k]], r4_recv.at[1, z_at[k]])

    right, left, far = (lax.rem(x + k, 4) for k in (1, 3, 2))
    to_right, to_left, to_other = (dp, 2 * right + core), (dp, 2 * left + core), (dp, 2 * x + other)
    g_right, g_left, g_far = 2 * right + core, 2 * left + core, 2 * far + core

    def pass_on(out, sem, block, slot, device):
        copy(out.at[block], out.at[block], x_send.at[sem, slot], x_recv.at[sem, slot], device)

    def swap(out, sem, block, slot):
        copy(out.at[block], out.at[block], c_send.at[sem, slot], c_recv.at[sem, slot], to_other)

    pass_on(out1, 0, g, 0, to_right)
    pass_on(out2, 1, g, 1, to_left)
    pass_on(out1, 0, g, 1, to_left)
    pass_on(out2, 1, g, 0, to_right)
    swap(out1, 0, g, 0)
    swap(out2, 1, g, 0)
    arrived(out1.at[g_left], x_recv.at[0, 0])
    pass_on(out1, 0, g_left, 2, to_right)
    arrived(out2.at[g_right], x_recv.at[1, 1])
    pass_on(out2, 1, g_right, 2, to_left)
    swap(out1, 0, g_left, 1)
    swap(out2, 1, g_right, 2)
    arrived(out1.at[g_right], x_recv.at[0, 1])
    swap(out1, 0, g_right, 2)
    arrived(out2.at[g_left], x_recv.at[1, 0])
    swap(out2, 1, g_left, 1)
    arrived(out1.at[g_far], x_recv.at[0, 2])
    swap(out1, 0, g_far, 3)
    arrived(out2.at[g_far], x_recv.at[1, 2])
    swap(out2, 1, g_far, 3)
    for slot, block in enumerate((x, left, right, far)):
        arrived(out1.at[2 * block + other], c_recv.at[0, slot])
        arrived(out2.at[2 * block + other], c_recv.at[1, slot])
    for c in sends:
        c.wait_send()


def place(updated_in, grad_atoms_in, out1, out2, updated, grad_atoms, grad_source, grad_output, sems):
    copies = [
        pltpu.make_async_copy(out2.at[i], grad_source.at[:, pl.ds(i * COLS, COLS)], sems.at[i]) for i in range(8)
    ]
    copies.append(pltpu.make_async_copy(out1, grad_output, sems.at[8]))
    copies.append(pltpu.make_async_copy(updated_in, updated, sems.at[9]))
    copies.append(pltpu.make_async_copy(grad_atoms_in, grad_atoms, sems.at[10]))
    for c in copies:
        c.start()
    for c in copies:
        c.wait()


def local(atoms, cotangent, sources, targets, radial, envelope, edge_counts, source_weight, radial_weight, output_weight):
    inputs = (atoms, cotangent, sources, targets, radial, envelope, source_weight, radial_weight, output_weight)
    hbm = pl.BlockSpec(memory_space=pltpu.HBM)
    vmem = pl.BlockSpec(memory_space=pltpu.VMEM)
    smem = pl.BlockSpec(memory_space=pltpu.SMEM)
    dma = pltpu.SemaphoreType.DMA
    updated, grad_atoms, out1, out2 = pl.pallas_call(
        body,
        out_shape=(
            pltpu.VMEM((1, OWN, DA), BF16),
            pltpu.VMEM((1, OWN, DA), BF16),
            pltpu.VMEM((8, SIDE, 16, DA), BF16),
            pltpu.VMEM((8, SIDE, 64, COLS), BF16),
        ),
        in_specs=[smem] + [hbm] * 9,
        out_specs=(vmem,) * 4,
        scratch_shapes=[pltpu.VMEM(a.shape, a.dtype) for a in inputs]
        + [
            pltpu.VMEM((8, SLOT, DA), BF16),
            pltpu.VMEM((2, ATOMS, DA), BF16),
            pltpu.VMEM((ATOMS, DE), BF16),
            pltpu.VMEM((EDGES, DA), BF16),
            pltpu.VMEM((EDGES, ATOMS), BF16),
            pltpu.VMEM((ATOMS, EDGES), BF16),
            pltpu.VMEM((ATOMS, EDGES), BF16),
            pltpu.VMEM((EDGES, 8), F32),
            pltpu.VMEM((EDGES, 2 * COLS), BF16),
            pltpu.VMEM((EDGES, 2 * COLS), BF16),
            pltpu.VMEM((4, 2, 2, ATOMS, COLS), BF16),
            pltpu.VMEM((8, 2, ATOMS, COLS), BF16),
            pltpu.VMEM((8, 2, PAD, COLS), BF16),
            pltpu.VMEM((2, PAD, DE), BF16),
            pltpu.VMEM((SIDE, 16, DA), BF16),
            pltpu.VMEM((SIDE, 64, COLS), BF16),
            pltpu.VMEM((SIDE, 16, DA), BF16),
            pltpu.VMEM((SIDE, 64, COLS), BF16),
            pltpu.VMEM((SIDE, 8, COLS), F32),
            pltpu.VMEM((SIDE, 8, COLS), F32),
            pltpu.VMEM((SIDE, 8, COLS), F32),
            pltpu.VMEM((SIDE, 8, COLS), F32),
            pltpu.VMEM((SIDE, 8, COLS), F32),
            pltpu.VMEM((SIDE, 8, COLS), F32),
            dma((8,)),
            dma((8,)),
            dma((8,)),
            dma((8,)),
            dma((8,)),
            dma((8,)),
            dma((2, SIDE)),
            dma((2, SIDE)),
            dma((2, SIDE)),
            dma((2, SIDE)),
            dma((2, SIDE)),
            dma((2, SIDE)),
            dma((2, SIDE)),
            dma((2, SIDE)),
            dma((2, 3)),
            dma((2, 3)),
            dma((2, 4)),
            dma((2, 4)),
            dma((9,)),
        ],
        compiler_params=pltpu.CompilerParams(
            collective_id=0, has_side_effects=True, vmem_limit_bytes=48 * 1024 * 1024
        ),
    )(edge_counts, *(pltpu.with_memory_space_constraint(a, pltpu.HBM) for a in inputs))
    results = (updated, grad_atoms, out1.reshape(DE, DA), out2.reshape(8, DA, COLS))
    return pl.pallas_call(
        place,
        out_shape=(
            jax.ShapeDtypeStruct((1, OWN, DA), BF16),
            jax.ShapeDtypeStruct((1, OWN, DA), BF16),
            jax.ShapeDtypeStruct((DA, DE), BF16),
            jax.ShapeDtypeStruct((DE, DA), BF16),
        ),
        in_specs=[vmem] * 4,
        out_specs=(hbm,) * 4,
        scratch_shapes=[dma((11,))],
    )(*(pltpu.with_memory_space_constraint(a, pltpu.VMEM) for a in results))


def solution(mesh):
    rows = P("dp", "graph", None)
    flat = P("dp", "graph")
    return jax.shard_map(
        local,
        mesh=mesh,
        in_specs=(rows, rows, flat, flat, rows, flat, flat, P(), P(), P()),
        out_specs=(rows, rows, P(), P()),
        check_vma=False,
    )
```

```python
import math

import jax
import jax.numpy as jnp
from jax import lax
from jax.experimental import pallas as pl
from jax.experimental.pallas import tpu as pltpu
from jax.sharding import PartitionSpec as P

MESH = pl.DeviceIdType.MESH
F32 = jnp.float32
BF16 = jnp.bfloat16

OWN = 24
ATOMS = 192
EDGES = 512
DA = 512
DE = 1024
NR = 128
PAD = 32
REST = 2 * OWN - PAD
COLS = 128
SIDE = 8
NEAR = (0, 1, 7, 2, 6, 3, 5, 4)
NEAR_X = (0, 1, 3, 2)
GROUPS = ((1, 3), (3, 5), (5, 8))
GROUPS_X = ((1, 3), (3, 4))


def dot(left, right):
    return jnp.dot(left, right, preferred_element_type=F32)


def dot_nt(left, right):
    return lax.dot_general(left, right, (((1,), (1,)), ((), ())), preferred_element_type=F32)


def dot_tn(left, right):
    return lax.dot_general(left, right, (((0,), (0,)), ((), ())), preferred_element_type=F32)


def hot(hit):
    return hit.astype(F32).astype(BF16)


def by_owner(index):
    return (index * 683) >> 14


def body(count_ref, *refs):
    inputs, refs = refs[:9], refs[9:]
    updated_ref, grad_atoms_ref, out1, out2 = refs[:4]
    (
        atoms_ref,
        cot_ref,
        src_ref,
        dst_ref,
        env_ref,
        ow_ref,
        left_s,
        right_s,
        full1,
        full2,
        atoms_s,
        atoms_t,
        cot_s,
        back_s,
        hot_src_s,
        hot_dst_s,
        hott_src_s,
        hott_dst_s,
        grow_s,
        cols_s,
        weight_s,
        pre_s,
        pulled_s,
        msg_s,
        dpre_s,
        keep,
        swap_out,
        swap_in,
        x_out,
        x_in,
        rows_out,
        rows_in,
        ga,
        gb,
        ra,
        rb,
        pa,
        pb,
        a1,
        a2,
        b1,
        b2,
        load_sem,
        full_send,
        full_recv,
        rs_send,
        rs_recv,
        row_send,
        row_recv,
        sum_send,
        sum_recv,
        g_send,
        near_recv,
        far_recv,
        core_recv,
    ) = refs[4:]
    dp = lax.axis_index("dp")
    g = lax.axis_index("graph")
    y, z = lax.div(dp, SIDE), lax.rem(dp, SIDE)
    x, core = lax.div(g, 2), lax.rem(g, 2)
    other = 1 - core
    scale = math.sqrt(OWN / EDGES)
    me = (dp, g)

    def send(src, dst, send_sem, recv_sem, device):
        pltpu.make_async_remote_copy(
            src_ref=src, dst_ref=dst, send_sem=send_sem, recv_sem=recv_sem, device_id=device, device_id_type=MESH
        ).start()

    def arrived(dst, sem):
        pltpu.make_async_remote_copy(
            src_ref=dst, dst_ref=dst, send_sem=sem, recv_sem=sem, device_id=me, device_id_type=MESH
        ).wait_recv()

    def sent(src, sem):
        pltpu.make_async_remote_copy(
            src_ref=src, dst_ref=src, send_sem=sem, recv_sem=sem, device_id=me, device_id_type=MESH
        ).wait_send()

    y_at = [lax.rem(y + k, SIDE) for k in range(SIDE)]
    z_at = [lax.rem(z + k, SIDE) for k in range(SIDE)]
    x_at = [lax.rem(x + k, 4) for k in range(4)]
    y_peer = [(y_at[k] * SIDE + z, g) for k in range(SIDE)]
    z_peer = [(y * SIDE + z_at[k], g) for k in range(SIDE)]
    x_peer = [(dp, 2 * x_at[k] + core) for k in range(4)]
    x_peer_other = [(dp, 2 * x_at[k] + other) for k in range(4)]
    sibling = x_peer_other[0]
    graph_peers = [x_peer[2], x_peer_other[2], x_peer[1], x_peer_other[1], x_peer[3], x_peer_other[3], sibling]

    barrier = pltpu.get_barrier_semaphore()
    for k in reversed(NEAR[1:]):
        for peer in (y_peer[k], z_peer[k]):
            pl.semaphore_signal(barrier, inc=1, device_id=peer, device_id_type=MESH)
    for peer in graph_peers:
        pl.semaphore_signal(barrier, inc=1, device_id=peer, device_id_type=MESH)

    places = (
        atoms_ref,
        cot_ref,
        src_ref,
        dst_ref,
        left_s.at[:, pl.ds(0, NR)],
        env_ref,
        right_s.at[pl.ds(NR, DA)],
        right_s.at[pl.ds(0, NR)],
        ow_ref,
    )
    loads = []
    for i, place in enumerate(places):
        held = inputs[i].at[0] if i == 4 else inputs[i]
        loads.append(pltpu.make_async_copy(held, place, load_sem.at[i]))
        loads[i].start()

    loads[0].wait()
    loads[1].wait()
    stacked = jnp.concatenate([atoms_ref[0], cot_ref[0]], axis=0)
    full1[g] = stacked[:PAD]
    full2[g] = stacked[PAD:]
    pl.semaphore_wait(barrier, 21)
    for peer in graph_peers:
        send(full1.at[g], full1.at[g], full_send.at[0], full_recv.at[0, g], peer)
    for peer in graph_peers:
        send(full2.at[g], full2.at[g], full_send.at[1], full_recv.at[1, g], peer)

    for i in (2, 3, 5):
        loads[i].wait()
    src_row = src_ref[...]
    dst_row = dst_ref[...]
    slots = lax.broadcasted_iota(jnp.int32, (1, EDGES), 1)
    live = (slots < count_ref[0, 0]).astype(F32)
    src_padded = src_row + (PAD - OWN) * by_owner(src_row)
    table = jnp.concatenate(
        [src_padded.astype(F32), dst_row.astype(F32), env_ref[...] * live, jnp.zeros((5, EDGES), F32)], axis=0
    )
    cols_s[...] = table.T
    hot_src_s[...] = hot(lax.broadcasted_iota(jnp.int32, (EDGES, 8 * PAD), 1).astype(F32) == cols_s[:, 0:1])
    hot_dst_s[...] = hot(lax.broadcasted_iota(jnp.int32, (EDGES, ATOMS), 1).astype(F32) == cols_s[:, 1:2])
    weight_s[...] = jnp.broadcast_to(cols_s[:, 2:3], (EDGES, COLS))
    atom_rows = lax.broadcasted_iota(jnp.int32, (ATOMS, EDGES), 0)
    hott_src_s[...] = hot(atom_rows == src_row)
    hott_dst_s[...] = hot(atom_rows == dst_row)
    at1_r = lax.broadcasted_iota(jnp.int32, (ATOMS, 8 * PAD), 0)
    at1_c = lax.broadcasted_iota(jnp.int32, (ATOMS, 8 * PAD), 1)
    at1 = at1_r + (PAD - OWN) * by_owner(at1_r)
    pick_atoms = hot(at1_c == at1)
    inner = at1_r - OWN * by_owner(at1_r)
    pick_cot1 = hot((at1_c == at1 + OWN) & (inner < PAD - OWN))
    at2_r = lax.broadcasted_iota(jnp.int32, (ATOMS, 8 * REST), 0)
    at2_c = lax.broadcasted_iota(jnp.int32, (ATOMS, 8 * REST), 1)
    owner2 = by_owner(at2_r)
    inner2 = at2_r - OWN * owner2
    pick_cot2 = hot((at2_c == owner2 * REST + inner2 - (PAD - OWN)) & (inner2 >= PAD - OWN))
    for i in (4, 6, 7, 8):
        loads[i].wait()

    for peer in graph_peers:
        arrived(full1.at[peer[1]], full_recv.at[0, peer[1]])
    both = full1[...].reshape(8 * PAD, DA)
    left_s[:, NR:] = dot(hot_src_s[...], both).astype(BF16)
    for peer in graph_peers:
        arrived(full2.at[peer[1]], full_recv.at[1, peer[1]])
    cot = (dot(pick_cot1, both) + dot(pick_cot2, full2[...].reshape(8 * REST, DA))).astype(BF16)
    cot_s[...] = cot
    back_s[...] = (dot_nt(cot, ow_ref[...]) * scale).astype(BF16)

    def pass_x(dx):
        arrived(swap_in.at[dx], rs_recv.at[0, dx])
        x_out[dx] = (keep[dx] + swap_in[dx].astype(F32)).astype(BF16)
        send(x_out.at[dx], x_in.at[dx], rs_send.at[1, dx], rs_recv.at[1, dx], x_peer[dx])

    before = None
    for dx in (2, 1, 3, 0):
        cols = pl.ds(pl.multiple_of(x_at[dx] * 2 * COLS, 2 * COLS), 2 * COLS)
        pre_s[...] = dot(left_s[...], right_s[:, cols])
        pulled_s[...] = dot(hot_dst_s[...], back_s[:, cols])
        for r in range(8):
            rows = slice(r * 64, (r + 1) * 64)
            pre = pre_s[rows, :]
            weight = jnp.concatenate([weight_s[rows, :]] * 2, axis=1)
            sigma = 0.5 * jnp.tanh(0.5 * pre) + 0.5
            silu = pre * sigma
            msg_s[rows, :] = (silu * weight).astype(BF16)
            slope = sigma + silu * (1.0 - sigma)
            dpre_s[rows, :] = (pulled_s[rows, :] * weight * slope).astype(BF16)
        for j, (picks, terms) in enumerate(((hott_dst_s, msg_s), (hott_src_s, dpre_s))):
            part = dot(picks[...], terms[...])
            low, high = part[:, :COLS], part[:, COLS:]
            keep[dx, j] = jnp.where(core == 0, low, high)
            swap_out[dx, j] = jnp.where(core == 0, high, low).astype(BF16)
        send(swap_out.at[dx], swap_in.at[dx], rs_send.at[0, dx], rs_recv.at[0, dx], sibling)
        if before:
            pass_x(before)
        before = dx

    atoms_s[...] = dot(pick_atoms, both).astype(BF16)
    atoms_t[...] = atoms_s[...].astype(F32).T.astype(BF16)
    grow_r = lax.broadcasted_iota(jnp.int32, (8 * PAD, ATOMS), 0)
    grow_c = lax.broadcasted_iota(jnp.int32, (8 * PAD, ATOMS), 1)
    inner = grow_r & (PAD - 1)
    grow_s[...] = hot((inner < OWN) & (grow_c == (grow_r >> 5) * OWN + inner))
    arrived(swap_in.at[0], rs_recv.at[0, 0])
    total = keep[0] + swap_in[0].astype(F32)
    for dx in (2, 1, 3):
        arrived(x_in.at[dx], rs_recv.at[1, dx])
        total = total + x_in[dx].astype(F32)
    sums = total.astype(BF16)
    summed, dsum = sums[0], sums[1]

    ga[...] = dot_tn(summed, cot_s[...]).astype(BF16).reshape(SIDE, 16, DA)
    gb[...] = dot(atoms_t[...], dsum).astype(BF16).reshape(SIDE, 64, COLS)
    for k in reversed(NEAR[1:]):
        send(ga.at[y_at[k]], ra.at[k], sum_send.at[0], sum_recv.at[0], y_peer[k])
        send(gb.at[z_at[k]], rb.at[k], sum_send.at[1], sum_recv.at[1], z_peer[k])

    rows_out[:, 0] = dot(grow_s[...], summed).astype(BF16).reshape(8, PAD, COLS)
    rows_out[:, 1] = dot(grow_s[...], dsum).astype(BF16).reshape(8, PAD, COLS)
    own_cols = pl.ds(pl.multiple_of(g * COLS, COLS), COLS)
    rows_in[:, :, own_cols] = rows_out[g]
    for peer in graph_peers:
        send(rows_out.at[peer[1]], rows_in.at[:, :, own_cols], row_send, row_recv.at[g], peer)

    arrived(ra.at[pl.ds(1, 7)], sum_recv.at[0])
    arrived(rb.at[pl.ds(1, 7)], sum_recv.at[1])
    sum_a = ga[y].astype(F32)
    sum_b = gb[z].astype(F32)
    for k in range(1, SIDE):
        sum_a = sum_a + ra[k].astype(F32)
        sum_b = sum_b + rb[k].astype(F32)

    pa[0] = sum_a.astype(BF16)
    pb[0] = sum_b.astype(BF16)
    for k in reversed(NEAR[1:]):
        send(pa.at[0], pa.at[k], sum_send.at[2], sum_recv.at[2], z_peer[k])
        send(pb.at[0], pb.at[k], sum_send.at[3], sum_recv.at[3], y_peer[k])

    for peer in graph_peers:
        peer_cols = pl.ds(pl.multiple_of(peer[1] * COLS, COLS), COLS)
        arrived(rows_in.at[:, :, peer_cols], row_recv.at[peer[1]])
    update = dot(rows_in[0], ow_ref[...]) * scale
    updated_ref[0] = (atoms_ref[0].astype(F32) + update[:OWN]).astype(BF16)
    pushed = dot_nt(rows_in[1], right_s[NR:, :])
    grad_atoms_ref[0] = (cot_ref[0].astype(F32) + pushed[:OWN]).astype(BF16)

    arrived(pa.at[pl.ds(1, 7)], sum_recv.at[2])
    arrived(pb.at[pl.ds(1, 7)], sum_recv.at[3])
    sum_a = pa[z].astype(F32)
    sum_b = pb[y].astype(F32)
    for j in range(1, SIDE):
        sum_a = sum_a + pa[lax.rem(z + SIDE - j, SIDE)].astype(F32)
        sum_b = sum_b + pb[lax.rem(y + SIDE - j, SIDE)].astype(F32)
    systems = SIDE * SIDE
    piece_a = (sum_a * (scale / math.sqrt(systems * ATOMS))).astype(BF16)
    piece_b = (sum_b * (16.0 / math.sqrt(systems * 8 * EDGES))).astype(BF16)
    a1[core, 0, 0] = piece_a[:, : DA // 2]
    a2[core, 0, 0] = piece_a[:, DA // 2 :]
    b1[core, 0, 0] = piece_b[:32]
    b2[core, 0, 0] = piece_b[32:]

    back_to = [[y_peer[(SIDE - k) % SIDE] for k in NEAR], [z_peer[(SIDE - k) % SIDE] for k in NEAR]]
    back_x = [x_peer[(4 - k) % 4] for k in NEAR_X]
    first = ((a1, 0, back_to[0]), (b1, 1, back_to[1]))
    second = ((a2, 2, back_to[0]), (b2, 3, back_to[1]))

    def group_of(s):
        return 0 if s < 3 else 1 if s < 5 else 2

    def pass_first(buf, n, lo, hi):
        for s in (3, 1, 2):
            send(
                buf.at[core, 0, pl.ds(lo, hi - lo)],
                buf.at[core, s, pl.ds(lo, hi - lo)],
                g_send.at[n, 1],
                far_recv.at[n, s - 1],
                back_x[s],
            )

    def pass_second(buf, n, peers, lo, hi):
        for s in range(7, 0, -1):
            send(
                buf.at[core, 0, pl.ds(lo, hi - lo)],
                buf.at[core, s, pl.ds(lo, hi - lo)],
                g_send.at[n, 1],
                far_recv.at[n, group_of(s)],
                peers[s],
            )

    def pass_core(buf, n, slot, lo, hi):
        send(
            buf.at[core, pl.ds(lo, hi - lo)],
            buf.at[core, pl.ds(lo, hi - lo)],
            g_send.at[n, 2],
            core_recv.at[n, slot],
            sibling,
        )

    for buf, n, peers in second:
        for s in (3, 1, 2):
            send(buf.at[core, 0, 0], buf.at[core, 0, s], g_send.at[n, 0], near_recv.at[n, 0 if s < 3 else 1], back_x[s])
    for buf, n, peers in first:
        for s in range(7, 0, -1):
            send(buf.at[core, 0, 0], buf.at[core, 0, s], g_send.at[n, 0], near_recv.at[n, group_of(s)], peers[s])
        pass_first(buf, n, 0, 1)
    for buf, n, peers in second:
        pass_second(buf, n, peers, 0, 1)
    for i in range(3):
        if i < 2:
            lo, hi = GROUPS_X[i]
            for buf, n, peers in second:
                arrived(buf.at[core, 0, pl.ds(lo, hi - lo)], near_recv.at[n, i])
                pass_second(buf, n, peers, lo, hi)
        lo, hi = GROUPS[i]
        for buf, n, peers in first:
            arrived(buf.at[core, 0, pl.ds(lo, hi - lo)], near_recv.at[n, i])
            pass_first(buf, n, lo, hi)
    for buf, n, peers in second + first:
        pass_core(buf, n, 0, 0, 1)

    def store(n, c, xs, ys):
        owner = 2 * x_at[NEAR_X[xs]] + c
        if n in (0, 2):
            piece = a1[c, xs, ys] if n == 0 else a2[c, ys, xs]
            half = slice(0, DA // 2) if n == 0 else slice(DA // 2, DA)
            out1[owner, y_at[NEAR[ys]], :, half] = piece
        else:
            piece = b1[c, xs, ys] if n == 1 else b2[c, ys, xs]
            rows = pl.ds(pl.multiple_of(z_at[NEAR[ys]] * 64 + (0 if n == 1 else 32), 32), 32)
            out2[rows, pl.ds(pl.multiple_of(owner * COLS, COLS), COLS)] = piece

    def store_all(n, c, lo, hi):
        for s in range(lo, hi):
            for t in range(8 if n < 2 else 4):
                if n < 2:
                    store(n, c, s, t)
                else:
                    store(n, c, t, s)

    for buf, n, peers in second + first:
        store_all(n, core, 0, 1)
    parts = []
    for i in range(3):
        for buf, n, peers in second:
            parts.append((buf, n, i, *GROUPS[i]))
        for buf, n, peers in first:
            parts.append((buf, n, i, i + 1, i + 2))
    for buf, n, i, lo, hi in parts:
        arrived(buf.at[core, pl.ds(lo, hi - lo)], far_recv.at[n, i])
        pass_core(buf, n, i + 1, lo, hi)
        store_all(n, core, lo, hi)
    for buf, n, peers in second + first:
        arrived(buf.at[other, pl.ds(0, 1)], core_recv.at[n, 0])
        store_all(n, other, 0, 1)
    for buf, n, i, lo, hi in parts:
        arrived(buf.at[other, pl.ds(lo, hi - lo)], core_recv.at[n, i + 1])
        store_all(n, other, lo, hi)

    for buf, n, peers in first + second:
        sent(buf.at[core, 0, pl.ds(1, 7 if n < 2 else 3)], g_send.at[n, 0])
        sent(buf.at[core, pl.ds(1, 3 if n < 2 else 7)], g_send.at[n, 1])
        sent(buf.at[core], g_send.at[n, 2])
    sent(full1.at[pl.ds(0, 7)], full_send.at[0])
    sent(full2.at[pl.ds(0, 7)], full_send.at[1])
    for dx in range(4):
        sent(swap_out.at[dx], rs_send.at[0, dx])
        if dx:
            sent(x_out.at[dx], rs_send.at[1, dx])
    sent(rows_out.at[pl.ds(0, 7)], row_send)
    sent(ra.at[pl.ds(1, 7)], sum_send.at[0])
    sent(rb.at[pl.ds(1, 7)], sum_send.at[1])
    sent(pa.at[pl.ds(1, 7)], sum_send.at[2])
    sent(pb.at[pl.ds(1, 7)], sum_send.at[3])


def place(*refs):
    sems = refs[8]
    copies = [pltpu.make_async_copy(refs[i], refs[4 + i], sems.at[i]) for i in range(4)]
    for c in copies:
        c.start()
    for c in copies:
        c.wait()


def local(atoms, cotangent, sources, targets, radial, envelope, edge_counts, source_weight, radial_weight, output_weight):
    inputs = (atoms, cotangent, sources, targets, radial, envelope, source_weight, radial_weight, output_weight)
    vmem = pl.BlockSpec(memory_space=pltpu.VMEM)
    smem = pl.BlockSpec(memory_space=pltpu.SMEM)
    hbm = pl.BlockSpec(memory_space=pltpu.HBM)
    dma = pltpu.SemaphoreType.DMA

    def like(a):
        return pltpu.VMEM(a.shape, a.dtype)

    updated, grad_atoms, out1, out2 = pl.pallas_call(
        body,
        out_shape=(
            pltpu.VMEM((1, OWN, DA), BF16),
            pltpu.VMEM((1, OWN, DA), BF16),
            pltpu.VMEM((8, SIDE, 16, DA), BF16),
            pltpu.VMEM((DA, DE), BF16),
        ),
        in_specs=[smem] + [hbm] * 9,
        out_specs=(vmem,) * 4,
        scratch_shapes=[
            like(atoms),
            like(cotangent),
            like(sources),
            like(targets),
            like(envelope),
            like(output_weight),
            pltpu.VMEM((EDGES, NR + DA), BF16),
            pltpu.VMEM((NR + DA, DE), BF16),
            pltpu.VMEM((8, PAD, DA), BF16),
            pltpu.VMEM((8, REST, DA), BF16),
            pltpu.VMEM((ATOMS, DA), BF16),
            pltpu.VMEM((DA, ATOMS), BF16),
            pltpu.VMEM((ATOMS, DA), BF16),
            pltpu.VMEM((ATOMS, DE), BF16),
            pltpu.VMEM((EDGES, 8 * PAD), BF16),
            pltpu.VMEM((EDGES, ATOMS), BF16),
            pltpu.VMEM((ATOMS, EDGES), BF16),
            pltpu.VMEM((ATOMS, EDGES), BF16),
            pltpu.VMEM((8 * PAD, ATOMS), BF16),
            pltpu.VMEM((EDGES, 8), F32),
            pltpu.VMEM((EDGES, COLS), F32),
            pltpu.VMEM((EDGES, 2 * COLS), F32),
            pltpu.VMEM((EDGES, 2 * COLS), F32),
            pltpu.VMEM((EDGES, 2 * COLS), BF16),
            pltpu.VMEM((EDGES, 2 * COLS), BF16),
            pltpu.VMEM((4, 2, ATOMS, COLS), F32),
            pltpu.VMEM((4, 2, ATOMS, COLS), BF16),
            pltpu.VMEM((4, 2, ATOMS, COLS), BF16),
            pltpu.VMEM((4, 2, ATOMS, COLS), BF16),
            pltpu.VMEM((4, 2, ATOMS, COLS), BF16),
            pltpu.VMEM((8, 2, PAD, COLS), BF16),
            pltpu.VMEM((2, PAD, DE), BF16),
            pltpu.VMEM((SIDE, 16, DA), BF16),
            pltpu.VMEM((SIDE, 64, COLS), BF16),
            pltpu.VMEM((SIDE, 16, DA), BF16),
            pltpu.VMEM((SIDE, 64, COLS), BF16),
            pltpu.VMEM((SIDE, 16, DA), BF16),
            pltpu.VMEM((SIDE, 64, COLS), BF16),
            pltpu.VMEM((2, 4, SIDE, 16, DA // 2), BF16),
            pltpu.VMEM((2, SIDE, 4, 16, DA // 2), BF16),
            pltpu.VMEM((2, 4, SIDE, 32, COLS), BF16),
            pltpu.VMEM((2, SIDE, 4, 32, COLS), BF16),
            dma((9,)),
            dma((2,)),
            dma((2, 8)),
            dma((2, 4)),
            dma((2, 4)),
            dma,
            dma((8,)),
            dma((4,)),
            dma((4,)),
            dma((4, 3)),
            dma((4, 3)),
            dma((4, 3)),
            dma((4, 4)),
        ],
        compiler_params=pltpu.CompilerParams(
            collective_id=0, has_side_effects=True, vmem_limit_bytes=48 * 1024 * 1024
        ),
    )(edge_counts, *(pltpu.with_memory_space_constraint(a, pltpu.HBM) for a in inputs))
    results = (updated, grad_atoms, out2, out1.reshape(DE, DA))
    return pl.pallas_call(
        place,
        out_shape=tuple(jax.ShapeDtypeStruct(a.shape, a.dtype) for a in results),
        in_specs=[vmem] * 4,
        out_specs=(hbm,) * 4,
        scratch_shapes=[dma((4,))],
    )(*(pltpu.with_memory_space_constraint(a, pltpu.VMEM) for a in results))


def solution(mesh):
    rows = P("dp", "graph", None)
    flat = P("dp", "graph")
    return jax.shard_map(
        local,
        mesh=mesh,
        in_specs=(rows, rows, flat, flat, rows, flat, flat, P(), P(), P()),
        out_specs=(rows, rows, P(), P()),
        check_vma=False,
    )
```

```python
import math

import jax
import jax.numpy as jnp
from jax import lax
from jax.experimental import pallas as pl
from jax.experimental.pallas import tpu as pltpu
from jax.sharding import PartitionSpec as P

MESH = pl.DeviceIdType.MESH
F32 = jnp.float32
BF16 = jnp.bfloat16

OWN = 24
ATOMS = 192
EDGES = 512
DA = 512
DE = 1024
NR = 128
SLOT = 2 * OWN
PAD = 32
COLS = 128
SIDE = 8
NEAR = (0, 1, 7, 2, 6, 3, 5, 4)
NEAR_X = (0, 1, 3, 2)
GROUPS = ((1, 3), (3, 5), (5, 8))
GROUPS_X = ((1, 3), (3, 4))


def dot(left, right):
    return jnp.dot(left, right, preferred_element_type=F32)


def dot_nt(left, right):
    return lax.dot_general(left, right, (((1,), (1,)), ((), ())), preferred_element_type=F32)


def dot_tn(left, right):
    return lax.dot_general(left, right, (((0,), (0,)), ((), ())), preferred_element_type=F32)


def hot(hit):
    return hit.astype(F32).astype(BF16)


def by_owner(index):
    return (index * 683) >> 14


def body(count_ref, *refs):
    inputs, refs = refs[:9], refs[9:]
    updated_ref, grad_atoms_ref, out1, out2 = refs[:4]
    (
        atoms_ref,
        cot_ref,
        src_ref,
        dst_ref,
        env_ref,
        ow_ref,
        rw_ref,
        sw_ref,
        basis,
        table,
        full,
        atoms_s,
        atoms_t,
        cot_s,
        rows_s,
        back_s,
        hot_src_s,
        hot_dst_s,
        hott_src_s,
        hott_dst_s,
        grow_s,
        weight_s,
        sum_s,
        rows_out,
        rows_in,
        ga,
        gb,
        ra,
        rb,
        pa,
        pb,
        a1,
        a2,
        b1,
        b2,
        load_sem,
        in_send,
        in_recv,
        row_send,
        row_recv,
        sum_send,
        sum_recv,
        g_send,
        near_recv,
        far_recv,
        core_recv,
    ) = refs[4:]
    dp = lax.axis_index("dp")
    g = lax.axis_index("graph")
    y, z = lax.div(dp, SIDE), lax.rem(dp, SIDE)
    x, core = lax.div(g, 2), lax.rem(g, 2)
    other = 1 - core
    scale = math.sqrt(OWN / EDGES)
    me = (dp, g)

    def send(src, dst, send_sem, recv_sem, device):
        pltpu.make_async_remote_copy(
            src_ref=src, dst_ref=dst, send_sem=send_sem, recv_sem=recv_sem, device_id=device, device_id_type=MESH
        ).start()

    def arrived(dst, sem):
        pltpu.make_async_remote_copy(
            src_ref=dst, dst_ref=dst, send_sem=sem, recv_sem=sem, device_id=me, device_id_type=MESH
        ).wait_recv()

    def sent(src, sem):
        pltpu.make_async_remote_copy(
            src_ref=src, dst_ref=src, send_sem=sem, recv_sem=sem, device_id=me, device_id_type=MESH
        ).wait_send()

    y_at = [lax.rem(y + k, SIDE) for k in range(SIDE)]
    z_at = [lax.rem(z + k, SIDE) for k in range(SIDE)]
    x_at = [lax.rem(x + k, 4) for k in range(4)]
    y_peer = [(y_at[k] * SIDE + z, g) for k in range(SIDE)]
    z_peer = [(y * SIDE + z_at[k], g) for k in range(SIDE)]
    x_peer = [(dp, 2 * x_at[k] + core) for k in range(4)]
    x_peer_other = [(dp, 2 * x_at[k] + other) for k in range(4)]
    sibling = x_peer_other[0]
    graph_peers = [x_peer[2], x_peer_other[2], x_peer[1], x_peer_other[1], x_peer[3], x_peer_other[3], sibling]

    barrier = pltpu.get_barrier_semaphore()
    for k in reversed(NEAR[1:]):
        for peer in (y_peer[k], z_peer[k]):
            pl.semaphore_signal(barrier, inc=1, device_id=peer, device_id_type=MESH)
    for peer in graph_peers:
        pl.semaphore_signal(barrier, inc=1, device_id=peer, device_id_type=MESH)

    held = (atoms_ref, cot_ref, src_ref, dst_ref, basis.at[g], env_ref, sw_ref, rw_ref, ow_ref)
    loads = []
    for i, ref in enumerate(held):
        source = inputs[i].at[0] if i == 4 else inputs[i]
        loads.append(pltpu.make_async_copy(source, ref, load_sem.at[i]))
    for i in (0, 1, 2, 3, 5, 4, 6, 7, 8):
        loads[i].start()

    loads[0].wait()
    loads[1].wait()
    full[g] = jnp.concatenate([atoms_ref[0], cot_ref[0]], axis=0)
    for i in (2, 3, 5):
        loads[i].wait()
    slots = lax.broadcasted_iota(jnp.int32, (1, EDGES), 1)
    live = (slots < count_ref[0, 0]).astype(F32)
    lines = (src_ref[...].astype(F32), dst_ref[...].astype(F32), env_ref[...] * live, jnp.zeros((1, EDGES), F32))
    table[g] = jnp.concatenate([line[:, j * 128 : (j + 1) * 128] for line in lines for j in range(4)], axis=0)
    loads[4].wait()
    pl.semaphore_wait(barrier, 21)
    gathered = (full, table, basis)

    def offer(n, k):
        buf = gathered[n]
        send(buf.at[g], buf.at[g], in_send.at[n, k], in_recv.at[n, g], x_peer[k] if k else sibling)

    for n in range(3):
        for k in (2, 1, 3, 0):
            if n < 2 or k != 2:
                offer(n, k)

    def block(k, c):
        return 2 * x_at[k] + c

    def relay(n, k):
        b = block(k, core)
        buf = gathered[n]
        arrived(buf.at[b], in_recv.at[n, b])
        send(buf.at[b], buf.at[b], in_send.at[n, 3 + k], in_recv.at[n, b], sibling)

    def select(b):
        lines = table[b]
        columns = lines.T
        row_atom = lax.broadcasted_iota(jnp.int32, (ATOMS, 128), 0).astype(F32)
        col_atom = lax.broadcasted_iota(jnp.int32, (128, ATOMS), 1).astype(F32)
        for j in range(4):
            edges = pl.ds(j * 128, 128)
            hot_src_s[b, edges, :] = hot(col_atom == columns[:, j : j + 1])
            hot_dst_s[b, edges, :] = hot(col_atom == columns[:, 4 + j : 5 + j])
            weight_s[b, edges, :] = jnp.broadcast_to(columns[:, 8 + j : 9 + j], (128, COLS))
            hott_src_s[b, :, edges] = hot(row_atom == lines[j : j + 1, :])
            hott_dst_s[b, :, edges] = hot(row_atom == lines[4 + j : 5 + j, :])

    select(g)
    pick_r = lax.broadcasted_iota(jnp.int32, (ATOMS, 8 * SLOT), 0)
    pick_c = lax.broadcasted_iota(jnp.int32, (ATOMS, 8 * SLOT), 1)
    pick_at = pick_r + OWN * by_owner(pick_r)
    pick_atoms = hot(pick_c == pick_at)
    pick_cot = hot(pick_c == pick_at + OWN)
    grow_r = lax.broadcasted_iota(jnp.int32, (8 * PAD, ATOMS), 0)
    grow_c = lax.broadcasted_iota(jnp.int32, (8 * PAD, ATOMS), 1)
    inner = grow_r & (PAD - 1)
    grow_s[...] = hot((inner < OWN) & (grow_c == (grow_r >> 5) * OWN + inner))
    for i in (6, 7, 8):
        loads[i].wait()
    for k in (1, 3, 2):
        relay(0, k)
    offer(2, 2)
    for k in (1, 3, 2):
        relay(1, k)
    for k in range(4):
        arrived(full.at[block(k, other)], in_recv.at[0, block(k, other)])
    both = full[...].reshape(8 * SLOT, DA)
    atoms = dot(pick_atoms, both).astype(BF16)
    cot = dot(pick_cot, both).astype(BF16)
    atoms_s[...] = atoms
    cot_s[...] = cot
    own_cols = pl.ds(pl.multiple_of(g * COLS, COLS), COLS)
    product = dot(atoms, sw_ref[:, own_cols])
    high = product.astype(BF16)
    rows_s[:, :COLS] = high
    rows_s[:, COLS:] = (product - high.astype(F32)).astype(BF16)
    back_s[...] = (dot_nt(cot, ow_ref[own_cols, :]) * scale).astype(BF16)

    def edges_of(b):
        at_src = dot(hot_src_s[b], rows_s[...])
        pre = dot(basis[b], rw_ref[:, own_cols]) + at_src[:, :COLS] + at_src[:, COLS:]
        pulled = dot(hot_dst_s[b], back_s[...])
        weight = weight_s[b]
        sigma = 0.5 * jnp.tanh(0.5 * pre) + 0.5
        silu = pre * sigma
        slope = sigma + silu * (1.0 - sigma)
        message = (silu * weight).astype(BF16)
        dpre = (pulled * weight * slope).astype(BF16)
        return dot(hott_dst_s[b], message), dot(hott_src_s[b], dpre)

    def add(b):
        first, second = edges_of(b)
        sum_s[0] += first
        sum_s[1] += second

    sum_s[0], sum_s[1] = edges_of(g)
    atoms_t[...] = atoms_s[...].astype(F32).T.astype(BF16)
    for k in (0, 1, 3, 2):
        if k:
            select(block(k, core))
        arrived(table.at[block(k, other)], in_recv.at[1, block(k, other)])
        select(block(k, other))
    arrived(basis.at[block(0, other)], in_recv.at[2, block(0, other)])
    add(block(0, other))
    for k in (1, 3):
        relay(2, k)
    add(block(1, core))
    add(block(3, core))
    for k in (1, 3):
        arrived(basis.at[block(k, other)], in_recv.at[2, block(k, other)])
        add(block(k, other))
    relay(2, 2)
    add(block(2, core))
    arrived(basis.at[block(2, other)], in_recv.at[2, block(2, other)])
    add(block(2, other))
    sums = sum_s[...].astype(BF16)
    summed, dsum = sums[0], sums[1]

    ga[...] = dot_tn(summed, cot_s[...]).astype(BF16).reshape(SIDE, 16, DA)
    gb[...] = dot(atoms_t[...], dsum).astype(BF16).reshape(SIDE, 64, COLS)
    for k in reversed(NEAR[1:]):
        send(ga.at[y_at[k]], ra.at[k], sum_send.at[0], sum_recv.at[0], y_peer[k])
        send(gb.at[z_at[k]], rb.at[k], sum_send.at[1], sum_recv.at[1], z_peer[k])

    rows_out[:, 0] = dot(grow_s[...], summed).astype(BF16).reshape(8, PAD, COLS)
    rows_out[:, 1] = dot(grow_s[...], dsum).astype(BF16).reshape(8, PAD, COLS)
    rows_in[:, :, own_cols] = rows_out[g]
    for peer in graph_peers:
        send(rows_out.at[peer[1]], rows_in.at[:, :, own_cols], row_send, row_recv.at[g], peer)

    arrived(ra.at[pl.ds(1, 7)], sum_recv.at[0])
    arrived(rb.at[pl.ds(1, 7)], sum_recv.at[1])
    sum_a = ga[y].astype(F32)
    sum_b = gb[z].astype(F32)
    for k in range(1, SIDE):
        sum_a = sum_a + ra[k].astype(F32)
        sum_b = sum_b + rb[k].astype(F32)

    pa[0] = sum_a.astype(BF16)
    pb[0] = sum_b.astype(BF16)
    for k in reversed(NEAR[1:]):
        send(pa.at[0], pa.at[k], sum_send.at[2], sum_recv.at[2], z_peer[k])
        send(pb.at[0], pb.at[k], sum_send.at[3], sum_recv.at[3], y_peer[k])

    for peer in graph_peers:
        peer_cols = pl.ds(pl.multiple_of(peer[1] * COLS, COLS), COLS)
        arrived(rows_in.at[:, :, peer_cols], row_recv.at[peer[1]])
    update = dot(rows_in[0], ow_ref[...]) * scale
    updated_ref[0] = (atoms_ref[0].astype(F32) + update[:OWN]).astype(BF16)
    pushed = dot_nt(rows_in[1], sw_ref[...])
    grad_atoms_ref[0] = (cot_ref[0].astype(F32) + pushed[:OWN]).astype(BF16)

    arrived(pa.at[pl.ds(1, 7)], sum_recv.at[2])
    arrived(pb.at[pl.ds(1, 7)], sum_recv.at[3])
    sum_a = pa[z].astype(F32)
    sum_b = pb[y].astype(F32)
    for j in range(1, SIDE):
        sum_a = sum_a + pa[lax.rem(z + SIDE - j, SIDE)].astype(F32)
        sum_b = sum_b + pb[lax.rem(y + SIDE - j, SIDE)].astype(F32)
    systems = SIDE * SIDE
    piece_a = (sum_a * (scale / math.sqrt(systems * ATOMS))).astype(BF16)
    piece_b = (sum_b * (16.0 / math.sqrt(systems * 8 * EDGES))).astype(BF16)
    a1[core, 0, 0] = piece_a[:, : DA // 2]
    a2[core, 0, 0] = piece_a[:, DA // 2 :]
    b1[core, 0, 0] = piece_b[:32]
    b2[core, 0, 0] = piece_b[32:]

    back_to = [[y_peer[(SIDE - k) % SIDE] for k in NEAR], [z_peer[(SIDE - k) % SIDE] for k in NEAR]]
    back_x = [x_peer[(4 - k) % 4] for k in NEAR_X]
    first = ((a1, 0, back_to[0]), (b1, 1, back_to[1]))
    second = ((a2, 2, back_to[0]), (b2, 3, back_to[1]))

    def group_of(s):
        return 0 if s < 3 else 1 if s < 5 else 2

    def pass_first(buf, n, lo, hi):
        for s in (3, 1, 2):
            send(
                buf.at[core, 0, pl.ds(lo, hi - lo)],
                buf.at[core, s, pl.ds(lo, hi - lo)],
                g_send.at[n, 1],
                far_recv.at[n, s - 1],
                back_x[s],
            )

    def pass_second(buf, n, peers, lo, hi):
        for s in range(7, 0, -1):
            send(
                buf.at[core, 0, pl.ds(lo, hi - lo)],
                buf.at[core, s, pl.ds(lo, hi - lo)],
                g_send.at[n, 1],
                far_recv.at[n, group_of(s)],
                peers[s],
            )

    def pass_core(buf, n, slot, lo, hi):
        send(
            buf.at[core, pl.ds(lo, hi - lo)],
            buf.at[core, pl.ds(lo, hi - lo)],
            g_send.at[n, 2],
            core_recv.at[n, slot],
            sibling,
        )

    for buf, n, peers in second:
        for s in (3, 1, 2):
            send(buf.at[core, 0, 0], buf.at[core, 0, s], g_send.at[n, 0], near_recv.at[n, 0 if s < 3 else 1], back_x[s])
    for buf, n, peers in first:
        for s in range(7, 0, -1):
            send(buf.at[core, 0, 0], buf.at[core, 0, s], g_send.at[n, 0], near_recv.at[n, group_of(s)], peers[s])
        pass_first(buf, n, 0, 1)
    for buf, n, peers in second:
        pass_second(buf, n, peers, 0, 1)
    for i in range(3):
        if i < 2:
            lo, hi = GROUPS_X[i]
            for buf, n, peers in second:
                arrived(buf.at[core, 0, pl.ds(lo, hi - lo)], near_recv.at[n, i])
                pass_second(buf, n, peers, lo, hi)
        lo, hi = GROUPS[i]
        for buf, n, peers in first:
            arrived(buf.at[core, 0, pl.ds(lo, hi - lo)], near_recv.at[n, i])
            pass_first(buf, n, lo, hi)
    for buf, n, peers in second + first:
        pass_core(buf, n, 0, 0, 1)

    def store(n, c, xs, ys):
        owner = 2 * x_at[NEAR_X[xs]] + c
        if n in (0, 2):
            piece = a1[c, xs, ys] if n == 0 else a2[c, ys, xs]
            half = slice(0, DA // 2) if n == 0 else slice(DA // 2, DA)
            out1[owner, y_at[NEAR[ys]], :, half] = piece
        else:
            piece = b1[c, xs, ys] if n == 1 else b2[c, ys, xs]
            rows = pl.ds(pl.multiple_of(z_at[NEAR[ys]] * 64 + (0 if n == 1 else 32), 32), 32)
            out2[rows, pl.ds(pl.multiple_of(owner * COLS, COLS), COLS)] = piece

    def store_all(n, c, lo, hi):
        for s in range(lo, hi):
            for t in range(8 if n < 2 else 4):
                if n < 2:
                    store(n, c, s, t)
                else:
                    store(n, c, t, s)

    for buf, n, peers in second + first:
        store_all(n, core, 0, 1)
    parts = []
    for i in range(3):
        for buf, n, peers in second:
            parts.append((buf, n, i, *GROUPS[i]))
        for buf, n, peers in first:
            parts.append((buf, n, i, i + 1, i + 2))
    for buf, n, i, lo, hi in parts:
        arrived(buf.at[core, pl.ds(lo, hi - lo)], far_recv.at[n, i])
        pass_core(buf, n, i + 1, lo, hi)
        store_all(n, core, lo, hi)
    for buf, n, peers in second + first:
        arrived(buf.at[other, pl.ds(0, 1)], core_recv.at[n, 0])
        store_all(n, other, 0, 1)
    for buf, n, i, lo, hi in parts:
        arrived(buf.at[other, pl.ds(lo, hi - lo)], core_recv.at[n, i + 1])
        store_all(n, other, lo, hi)

    for buf, n, peers in first + second:
        sent(buf.at[core, 0, pl.ds(1, 7 if n < 2 else 3)], g_send.at[n, 0])
        sent(buf.at[core, pl.ds(1, 3 if n < 2 else 7)], g_send.at[n, 1])
        sent(buf.at[core], g_send.at[n, 2])
    for n, buf in enumerate(gathered):
        for k in range(7):
            sent(buf.at[0], in_send.at[n, k])
    sent(rows_out.at[pl.ds(0, 7)], row_send)
    sent(ra.at[pl.ds(1, 7)], sum_send.at[0])
    sent(rb.at[pl.ds(1, 7)], sum_send.at[1])
    sent(pa.at[pl.ds(1, 7)], sum_send.at[2])
    sent(pb.at[pl.ds(1, 7)], sum_send.at[3])


def place(*refs):
    sems = refs[8]
    copies = [pltpu.make_async_copy(refs[i], refs[4 + i], sems.at[i]) for i in range(4)]
    for c in copies:
        c.start()
    for c in copies:
        c.wait()


def local(atoms, cotangent, sources, targets, radial, envelope, edge_counts, source_weight, radial_weight, output_weight):
    inputs = (atoms, cotangent, sources, targets, radial, envelope, source_weight, radial_weight, output_weight)
    vmem = pl.BlockSpec(memory_space=pltpu.VMEM)
    hbm = pl.BlockSpec(memory_space=pltpu.HBM)
    smem = pl.BlockSpec(memory_space=pltpu.SMEM)
    dma = pltpu.SemaphoreType.DMA

    def like(a):
        return pltpu.VMEM(a.shape, a.dtype)

    updated, grad_atoms, out1, out2 = pl.pallas_call(
        body,
        out_shape=(
            pltpu.VMEM((1, OWN, DA), BF16),
            pltpu.VMEM((1, OWN, DA), BF16),
            pltpu.VMEM((8, SIDE, 16, DA), BF16),
            pltpu.VMEM((DA, DE), BF16),
        ),
        in_specs=[smem] + [hbm] * 9,
        out_specs=(vmem,) * 4,
        scratch_shapes=[
            like(atoms),
            like(cotangent),
            like(sources),
            like(targets),
            like(envelope),
            like(output_weight),
            like(radial_weight),
            like(source_weight),
            pltpu.VMEM((8, EDGES, NR), BF16),
            pltpu.VMEM((8, 16, 128), F32),
            pltpu.VMEM((8, SLOT, DA), BF16),
            pltpu.VMEM((ATOMS, DA), BF16),
            pltpu.VMEM((DA, ATOMS), BF16),
            pltpu.VMEM((ATOMS, DA), BF16),
            pltpu.VMEM((ATOMS, 2 * COLS), BF16),
            pltpu.VMEM((ATOMS, COLS), BF16),
            pltpu.VMEM((8, EDGES, ATOMS), BF16),
            pltpu.VMEM((8, EDGES, ATOMS), BF16),
            pltpu.VMEM((8, ATOMS, EDGES), BF16),
            pltpu.VMEM((8, ATOMS, EDGES), BF16),
            pltpu.VMEM((8 * PAD, ATOMS), BF16),
            pltpu.VMEM((8, EDGES, COLS), F32),
            pltpu.VMEM((2, ATOMS, COLS), F32),
            pltpu.VMEM((8, 2, PAD, COLS), BF16),
            pltpu.VMEM((2, PAD, DE), BF16),
            pltpu.VMEM((SIDE, 16, DA), BF16),
            pltpu.VMEM((SIDE, 64, COLS), BF16),
            pltpu.VMEM((SIDE, 16, DA), BF16),
            pltpu.VMEM((SIDE, 64, COLS), BF16),
            pltpu.VMEM((SIDE, 16, DA), BF16),
            pltpu.VMEM((SIDE, 64, COLS), BF16),
            pltpu.VMEM((2, 4, SIDE, 16, DA // 2), BF16),
            pltpu.VMEM((2, SIDE, 4, 16, DA // 2), BF16),
            pltpu.VMEM((2, 4, SIDE, 32, COLS), BF16),
            pltpu.VMEM((2, SIDE, 4, 32, COLS), BF16),
            dma((9,)),
            dma((3, 7)),
            dma((3, 8)),
            dma,
            dma((8,)),
            dma((4,)),
            dma((4,)),
            dma((4, 3)),
            dma((4, 3)),
            dma((4, 3)),
            dma((4, 4)),
        ],
        compiler_params=pltpu.CompilerParams(
            collective_id=0, has_side_effects=True, vmem_limit_bytes=48 * 1024 * 1024
        ),
    )(edge_counts, *(pltpu.with_memory_space_constraint(a, pltpu.HBM) for a in inputs))
    results = (updated, grad_atoms, out2, out1.reshape(DE, DA))
    return pl.pallas_call(
        place,
        out_shape=tuple(jax.ShapeDtypeStruct(a.shape, a.dtype) for a in results),
        in_specs=[vmem] * 4,
        out_specs=(hbm,) * 4,
        scratch_shapes=[dma((4,))],
    )(*(pltpu.with_memory_space_constraint(a, pltpu.VMEM) for a in results))


def solution(mesh):
    rows = P("dp", "graph", None)
    flat = P("dp", "graph")
    return jax.shard_map(
        local,
        mesh=mesh,
        in_specs=(rows, rows, flat, flat, rows, flat, flat, P(), P(), P()),
        out_specs=(rows, rows, P(), P()),
        check_vma=False,
    )
```

```python
import math

import jax
import jax.numpy as jnp
from jax import lax
from jax.experimental import pallas as pl
from jax.experimental.pallas import tpu as pltpu
from jax.sharding import PartitionSpec as P

MESH = pl.DeviceIdType.MESH
F32 = jnp.float32
BF16 = jnp.bfloat16

OWN = 24
ATOMS = 192
EDGES = 512
DA = 512
DE = 1024
NR = 128
SLOT = 2 * OWN
PAD = 32
COLS = 128
SIDE = 8
NEAR = (0, 1, 7, 2, 6, 3, 5, 4)
NEAR_X = (0, 1, 3, 2)
GROUPS = ((1, 3), (3, 5), (5, 8))
GROUPS_X = ((1, 3), (3, 4))


def dot(left, right):
    return jnp.dot(left, right, preferred_element_type=F32)


def dot_nt(left, right):
    return lax.dot_general(left, right, (((1,), (1,)), ((), ())), preferred_element_type=F32)


def dot_tn(left, right):
    return lax.dot_general(left, right, (((0,), (0,)), ((), ())), preferred_element_type=F32)


def hot(hit):
    return hit.astype(F32).astype(BF16)


def by_owner(index):
    return (index * 683) >> 14


def body(count_ref, *refs):
    inputs, refs = refs[:9], refs[9:]
    updated_ref, grad_atoms_ref, out1, out2 = refs[:4]
    (
        atoms_ref,
        cot_ref,
        src_ref,
        dst_ref,
        env_ref,
        ow_ref,
        rw_ref,
        sw_ref,
        basis,
        table,
        full,
        atoms_s,
        atoms_t,
        cot_s,
        rows_s,
        back_s,
        hot_src_s,
        hot_dst_s,
        hott_src_s,
        hott_dst_s,
        grow_s,
        weight_s,
        sum_s,
        rows_out,
        rows_in,
        ga,
        gb,
        ra,
        rb,
        pa,
        pb,
        a1,
        a2,
        b1,
        b2,
        load_sem,
        in_send,
        in_recv,
        row_send,
        row_recv,
        sum_send,
        sum_recv,
        g_send,
        near_recv,
        far_recv,
        core_recv,
    ) = refs[4:]
    dp = lax.axis_index("dp")
    g = lax.axis_index("graph")
    y, z = lax.div(dp, SIDE), lax.rem(dp, SIDE)
    x, core = lax.div(g, 2), lax.rem(g, 2)
    other = 1 - core
    scale = math.sqrt(OWN / EDGES)
    me = (dp, g)

    def send(src, dst, send_sem, recv_sem, device):
        pltpu.make_async_remote_copy(
            src_ref=src, dst_ref=dst, send_sem=send_sem, recv_sem=recv_sem, device_id=device, device_id_type=MESH
        ).start()

    def arrived(dst, sem):
        pltpu.make_async_remote_copy(
            src_ref=dst, dst_ref=dst, send_sem=sem, recv_sem=sem, device_id=me, device_id_type=MESH
        ).wait_recv()

    def sent(src, sem):
        pltpu.make_async_remote_copy(
            src_ref=src, dst_ref=src, send_sem=sem, recv_sem=sem, device_id=me, device_id_type=MESH
        ).wait_send()

    y_at = [lax.rem(y + k, SIDE) for k in range(SIDE)]
    z_at = [lax.rem(z + k, SIDE) for k in range(SIDE)]
    x_at = [lax.rem(x + k, 4) for k in range(4)]
    y_peer = [(y_at[k] * SIDE + z, g) for k in range(SIDE)]
    z_peer = [(y * SIDE + z_at[k], g) for k in range(SIDE)]
    x_peer = [(dp, 2 * x_at[k] + core) for k in range(4)]
    x_peer_other = [(dp, 2 * x_at[k] + other) for k in range(4)]
    sibling = x_peer_other[0]
    graph_peers = [x_peer[2], x_peer_other[2], x_peer[1], x_peer_other[1], x_peer[3], x_peer_other[3], sibling]

    barrier = pltpu.get_barrier_semaphore()
    for peer in graph_peers:
        pl.semaphore_signal(barrier, inc=1, device_id=peer, device_id_type=MESH)
    held = (atoms_ref, cot_ref, src_ref, dst_ref, basis.at[g], env_ref, sw_ref, rw_ref, ow_ref)
    loads = []
    for i, ref in enumerate(held):
        source = inputs[i].at[0] if i == 4 else inputs[i]
        loads.append(pltpu.make_async_copy(source, ref, load_sem.at[i]))
    for i in (0, 1, 2, 3, 5, 4, 6, 7, 8):
        loads[i].start()
    for k in reversed(NEAR[1:]):
        for peer in (y_peer[k], z_peer[k]):
            pl.semaphore_signal(barrier, inc=1, device_id=peer, device_id_type=MESH)

    loads[0].wait()
    loads[1].wait()
    full[g] = jnp.concatenate([atoms_ref[0], cot_ref[0]], axis=0)
    for i in (2, 3, 5):
        loads[i].wait()
    slots = lax.broadcasted_iota(jnp.int32, (1, EDGES), 1)
    live = (slots < count_ref[0, 0]).astype(F32)
    lines = (src_ref[...].astype(F32), dst_ref[...].astype(F32), env_ref[...] * live, jnp.zeros((1, EDGES), F32))
    table[g] = jnp.concatenate([line[:, j * 128 : (j + 1) * 128] for line in lines for j in range(4)], axis=0)
    loads[4].wait()
    pl.semaphore_wait(barrier, 21)
    gathered = (full, table, basis)

    def offer(n, k):
        buf = gathered[n]
        send(buf.at[g], buf.at[g], in_send.at[n, k], in_recv.at[n, g], x_peer[k] if k else sibling)

    for n in (1, 0, 2):
        for k in (2, 1, 3, 0):
            if n < 2 or k != 2:
                offer(n, k)

    def block(k, c):
        return 2 * x_at[k] + c

    def relay(n, k):
        b = block(k, core)
        buf = gathered[n]
        arrived(buf.at[b], in_recv.at[n, b])
        send(buf.at[b], buf.at[b], in_send.at[n, 3 + k], in_recv.at[n, b], sibling)

    def select(b):
        lines = table[b]
        columns = lines.T
        row_atom = lax.broadcasted_iota(jnp.int32, (ATOMS, 128), 0).astype(F32)
        col_atom = lax.broadcasted_iota(jnp.int32, (128, ATOMS), 1).astype(F32)
        for j in range(4):
            edges = pl.ds(j * 128, 128)
            hot_src_s[b, edges, :] = hot(col_atom == columns[:, j : j + 1])
            hot_dst_s[b, edges, :] = hot(col_atom == columns[:, 4 + j : 5 + j])
            weight_s[b, edges, :] = jnp.broadcast_to(columns[:, 8 + j : 9 + j], (128, COLS))
            hott_src_s[b, :, edges] = hot(row_atom == lines[j : j + 1, :])
            hott_dst_s[b, :, edges] = hot(row_atom == lines[4 + j : 5 + j, :])

    select(g)
    pick_r = lax.broadcasted_iota(jnp.int32, (ATOMS, 8 * SLOT), 0)
    pick_c = lax.broadcasted_iota(jnp.int32, (ATOMS, 8 * SLOT), 1)
    pick_at = pick_r + OWN * by_owner(pick_r)
    pick_atoms = hot(pick_c == pick_at)
    pick_cot = hot(pick_c == pick_at + OWN)
    grow_r = lax.broadcasted_iota(jnp.int32, (8 * PAD, ATOMS), 0)
    grow_c = lax.broadcasted_iota(jnp.int32, (8 * PAD, ATOMS), 1)
    inner = grow_r & (PAD - 1)
    grow_s[...] = hot((inner < OWN) & (grow_c == (grow_r >> 5) * OWN + inner))
    arrived(table.at[block(0, other)], in_recv.at[1, block(0, other)])
    select(block(0, other))
    offer(2, 2)
    for k in (1, 3, 2):
        relay(1, k)
    for k in (1, 3, 2):
        select(block(k, core))
        relay(0, k)
    for k in (1, 3, 2):
        arrived(table.at[block(k, other)], in_recv.at[1, block(k, other)])
        select(block(k, other))
    for i in (6, 7, 8):
        loads[i].wait()
    for k in range(4):
        arrived(full.at[block(k, other)], in_recv.at[0, block(k, other)])
    both = full[...].reshape(8 * SLOT, DA)
    atoms = dot(pick_atoms, both).astype(BF16)
    cot = dot(pick_cot, both).astype(BF16)
    atoms_s[...] = atoms
    cot_s[...] = cot
    own_cols = pl.ds(pl.multiple_of(g * COLS, COLS), COLS)
    product = dot(atoms, sw_ref[:, own_cols])
    high = product.astype(BF16)
    rows_s[:, :COLS] = high
    rows_s[:, COLS:] = (product - high.astype(F32)).astype(BF16)
    back_s[...] = (dot_nt(cot, ow_ref[own_cols, :]) * scale).astype(BF16)

    def edges_of(b):
        at_src = dot(hot_src_s[b], rows_s[...])
        pre = dot(basis[b], rw_ref[:, own_cols]) + at_src[:, :COLS] + at_src[:, COLS:]
        pulled = dot(hot_dst_s[b], back_s[...])
        weight = weight_s[b]
        sigma = 0.5 * jnp.tanh(0.5 * pre) + 0.5
        silu = pre * sigma
        slope = sigma + silu * (1.0 - sigma)
        message = (silu * weight).astype(BF16)
        dpre = (pulled * weight * slope).astype(BF16)
        return dot(hott_dst_s[b], message), dot(hott_src_s[b], dpre)

    def add(b):
        first, second = edges_of(b)
        sum_s[0] += first
        sum_s[1] += second

    sum_s[0], sum_s[1] = edges_of(g)
    arrived(basis.at[block(0, other)], in_recv.at[2, block(0, other)])
    add(block(0, other))
    for k in (1, 3):
        relay(2, k)
    add(block(1, core))
    add(block(3, core))
    atoms_t[...] = atoms_s[...].astype(F32).T.astype(BF16)
    for k in (1, 3):
        arrived(basis.at[block(k, other)], in_recv.at[2, block(k, other)])
        add(block(k, other))
    relay(2, 2)
    add(block(2, core))
    arrived(basis.at[block(2, other)], in_recv.at[2, block(2, other)])
    add(block(2, other))
    sums = sum_s[...].astype(BF16)
    summed, dsum = sums[0], sums[1]

    ga[...] = dot_tn(summed, cot_s[...]).astype(BF16).reshape(SIDE, 16, DA)
    gb[...] = dot(atoms_t[...], dsum).astype(BF16).reshape(SIDE, 64, COLS)
    for k in reversed(NEAR[1:]):
        send(ga.at[y_at[k]], ra.at[k], sum_send.at[0], sum_recv.at[0], y_peer[k])
        send(gb.at[z_at[k]], rb.at[k], sum_send.at[1], sum_recv.at[1], z_peer[k])

    rows_out[:, 0] = dot(grow_s[...], summed).astype(BF16).reshape(8, PAD, COLS)
    rows_out[:, 1] = dot(grow_s[...], dsum).astype(BF16).reshape(8, PAD, COLS)
    rows_in[:, :, own_cols] = rows_out[g]
    for peer in graph_peers:
        send(rows_out.at[peer[1]], rows_in.at[:, :, own_cols], row_send, row_recv.at[g], peer)

    arrived(ra.at[pl.ds(1, 7)], sum_recv.at[0])
    arrived(rb.at[pl.ds(1, 7)], sum_recv.at[1])
    sum_a = ga[y].astype(F32)
    sum_b = gb[z].astype(F32)
    for k in range(1, SIDE):
        sum_a = sum_a + ra[k].astype(F32)
        sum_b = sum_b + rb[k].astype(F32)

    pa[0] = sum_a.astype(BF16)
    pb[0] = sum_b.astype(BF16)
    for k in reversed(NEAR[1:]):
        send(pa.at[0], pa.at[k], sum_send.at[2], sum_recv.at[2], z_peer[k])
        send(pb.at[0], pb.at[k], sum_send.at[3], sum_recv.at[3], y_peer[k])

    for peer in graph_peers:
        peer_cols = pl.ds(pl.multiple_of(peer[1] * COLS, COLS), COLS)
        arrived(rows_in.at[:, :, peer_cols], row_recv.at[peer[1]])
    update = dot(rows_in[0], ow_ref[...]) * scale
    updated_ref[0] = (atoms_ref[0].astype(F32) + update[:OWN]).astype(BF16)
    pushed = dot_nt(rows_in[1], sw_ref[...])
    grad_atoms_ref[0] = (cot_ref[0].astype(F32) + pushed[:OWN]).astype(BF16)

    arrived(pa.at[pl.ds(1, 7)], sum_recv.at[2])
    arrived(pb.at[pl.ds(1, 7)], sum_recv.at[3])
    sum_a = pa[z].astype(F32)
    sum_b = pb[y].astype(F32)
    for j in range(1, SIDE):
        sum_a = sum_a + pa[lax.rem(z + SIDE - j, SIDE)].astype(F32)
        sum_b = sum_b + pb[lax.rem(y + SIDE - j, SIDE)].astype(F32)
    systems = SIDE * SIDE
    piece_a = (sum_a * (scale / math.sqrt(systems * ATOMS))).astype(BF16)
    piece_b = (sum_b * (16.0 / math.sqrt(systems * 8 * EDGES))).astype(BF16)
    a1[core, 0, 0] = piece_a[:, : DA // 2]
    a2[core, 0, 0] = piece_a[:, DA // 2 :]
    b1[core, 0, 0] = piece_b[:32]
    b2[core, 0, 0] = piece_b[32:]

    back_to = [[y_peer[(SIDE - k) % SIDE] for k in NEAR], [z_peer[(SIDE - k) % SIDE] for k in NEAR]]
    back_x = [x_peer[(4 - k) % 4] for k in NEAR_X]
    first = ((a1, 0, back_to[0]), (b1, 1, back_to[1]))
    second = ((a2, 2, back_to[0]), (b2, 3, back_to[1]))

    def group_of(s):
        return 0 if s < 3 else 1 if s < 5 else 2

    def pass_first(buf, n, lo, hi):
        for s in (3, 1, 2):
            send(
                buf.at[core, 0, pl.ds(lo, hi - lo)],
                buf.at[core, s, pl.ds(lo, hi - lo)],
                g_send.at[n, 1],
                far_recv.at[n, s - 1],
                back_x[s],
            )

    def pass_second(buf, n, peers, lo, hi):
        for s in range(7, 0, -1):
            send(
                buf.at[core, 0, pl.ds(lo, hi - lo)],
                buf.at[core, s, pl.ds(lo, hi - lo)],
                g_send.at[n, 1],
                far_recv.at[n, group_of(s)],
                peers[s],
            )

    def pass_core(buf, n, slot, lo, hi):
        send(
            buf.at[core, pl.ds(lo, hi - lo)],
            buf.at[core, pl.ds(lo, hi - lo)],
            g_send.at[n, 2],
            core_recv.at[n, slot],
            sibling,
        )

    for buf, n, peers in second:
        for s in (3, 1, 2):
            send(buf.at[core, 0, 0], buf.at[core, 0, s], g_send.at[n, 0], near_recv.at[n, 0 if s < 3 else 1], back_x[s])
    for buf, n, peers in first:
        for s in range(7, 0, -1):
            send(buf.at[core, 0, 0], buf.at[core, 0, s], g_send.at[n, 0], near_recv.at[n, group_of(s)], peers[s])
        pass_first(buf, n, 0, 1)
    for buf, n, peers in second:
        pass_second(buf, n, peers, 0, 1)
    for i in range(3):
        if i < 2:
            lo, hi = GROUPS_X[i]
            for buf, n, peers in second:
                arrived(buf.at[core, 0, pl.ds(lo, hi - lo)], near_recv.at[n, i])
                pass_second(buf, n, peers, lo, hi)
        lo, hi = GROUPS[i]
        for buf, n, peers in first:
            arrived(buf.at[core, 0, pl.ds(lo, hi - lo)], near_recv.at[n, i])
            pass_first(buf, n, lo, hi)
    for buf, n, peers in second + first:
        pass_core(buf, n, 0, 0, 1)

    def store(n, c, xs, ys):
        owner = 2 * x_at[NEAR_X[xs]] + c
        if n in (0, 2):
            piece = a1[c, xs, ys] if n == 0 else a2[c, ys, xs]
            half = slice(0, DA // 2) if n == 0 else slice(DA // 2, DA)
            out1[owner, y_at[NEAR[ys]], :, half] = piece
        else:
            piece = b1[c, xs, ys] if n == 1 else b2[c, ys, xs]
            rows = pl.ds(pl.multiple_of(z_at[NEAR[ys]] * 64 + (0 if n == 1 else 32), 32), 32)
            out2[rows, pl.ds(pl.multiple_of(owner * COLS, COLS), COLS)] = piece

    def store_all(n, c, lo, hi):
        for s in range(lo, hi):
            for t in range(8 if n < 2 else 4):
                if n < 2:
                    store(n, c, s, t)
                else:
                    store(n, c, t, s)

    for buf, n, peers in second + first:
        store_all(n, core, 0, 1)
    parts = []
    for i in range(3):
        for buf, n, peers in second:
            parts.append((buf, n, i, *GROUPS[i]))
        for buf, n, peers in first:
            parts.append((buf, n, i, i + 1, i + 2))
    for buf, n, i, lo, hi in parts:
        arrived(buf.at[core, pl.ds(lo, hi - lo)], far_recv.at[n, i])
        pass_core(buf, n, i + 1, lo, hi)
        store_all(n, core, lo, hi)
    for buf, n, peers in second + first:
        arrived(buf.at[other, pl.ds(0, 1)], core_recv.at[n, 0])
        store_all(n, other, 0, 1)
    for buf, n, i, lo, hi in parts:
        arrived(buf.at[other, pl.ds(lo, hi - lo)], core_recv.at[n, i + 1])
        store_all(n, other, lo, hi)

    for buf, n, peers in first + second:
        sent(buf.at[core, 0, pl.ds(1, 7 if n < 2 else 3)], g_send.at[n, 0])
        sent(buf.at[core, pl.ds(1, 3 if n < 2 else 7)], g_send.at[n, 1])
        sent(buf.at[core], g_send.at[n, 2])
    for n, buf in enumerate(gathered):
        for k in range(7):
            sent(buf.at[0], in_send.at[n, k])
    sent(rows_out.at[pl.ds(0, 7)], row_send)
    sent(ra.at[pl.ds(1, 7)], sum_send.at[0])
    sent(rb.at[pl.ds(1, 7)], sum_send.at[1])
    sent(pa.at[pl.ds(1, 7)], sum_send.at[2])
    sent(pb.at[pl.ds(1, 7)], sum_send.at[3])


def place(*refs):
    sems = refs[8]
    copies = [pltpu.make_async_copy(refs[i], refs[4 + i], sems.at[i]) for i in range(2)]
    for i in (2, 3):
        rows = refs[i].shape[0] // 8
        for j in range(8):
            part = pl.ds(j * rows, rows)
            copies.append(pltpu.make_async_copy(refs[i].at[part], refs[4 + i].at[part], sems.at[len(copies)]))
    for c in copies:
        c.start()
    for c in copies:
        c.wait()


def local(atoms, cotangent, sources, targets, radial, envelope, edge_counts, source_weight, radial_weight, output_weight):
    inputs = (atoms, cotangent, sources, targets, radial, envelope, source_weight, radial_weight, output_weight)
    vmem = pl.BlockSpec(memory_space=pltpu.VMEM)
    hbm = pl.BlockSpec(memory_space=pltpu.HBM)
    smem = pl.BlockSpec(memory_space=pltpu.SMEM)
    dma = pltpu.SemaphoreType.DMA

    def like(a):
        return pltpu.VMEM(a.shape, a.dtype)

    updated, grad_atoms, out1, out2 = pl.pallas_call(
        body,
        out_shape=(
            pltpu.VMEM((1, OWN, DA), BF16),
            pltpu.VMEM((1, OWN, DA), BF16),
            pltpu.VMEM((8, SIDE, 16, DA), BF16),
            pltpu.VMEM((DA, DE), BF16),
        ),
        in_specs=[smem] + [hbm] * 9,
        out_specs=(vmem,) * 4,
        scratch_shapes=[
            like(atoms),
            like(cotangent),
            like(sources),
            like(targets),
            like(envelope),
            like(output_weight),
            like(radial_weight),
            like(source_weight),
            pltpu.VMEM((8, EDGES, NR), BF16),
            pltpu.VMEM((8, 16, 128), F32),
            pltpu.VMEM((8, SLOT, DA), BF16),
            pltpu.VMEM((ATOMS, DA), BF16),
            pltpu.VMEM((DA, ATOMS), BF16),
            pltpu.VMEM((ATOMS, DA), BF16),
            pltpu.VMEM((ATOMS, 2 * COLS), BF16),
            pltpu.VMEM((ATOMS, COLS), BF16),
            pltpu.VMEM((8, EDGES, ATOMS), BF16),
            pltpu.VMEM((8, EDGES, ATOMS), BF16),
            pltpu.VMEM((8, ATOMS, EDGES), BF16),
            pltpu.VMEM((8, ATOMS, EDGES), BF16),
            pltpu.VMEM((8 * PAD, ATOMS), BF16),
            pltpu.VMEM((8, EDGES, COLS), F32),
            pltpu.VMEM((2, ATOMS, COLS), F32),
            pltpu.VMEM((8, 2, PAD, COLS), BF16),
            pltpu.VMEM((2, PAD, DE), BF16),
            pltpu.VMEM((SIDE, 16, DA), BF16),
            pltpu.VMEM((SIDE, 64, COLS), BF16),
            pltpu.VMEM((SIDE, 16, DA), BF16),
            pltpu.VMEM((SIDE, 64, COLS), BF16),
            pltpu.VMEM((SIDE, 16, DA), BF16),
            pltpu.VMEM((SIDE, 64, COLS), BF16),
            pltpu.VMEM((2, 4, SIDE, 16, DA // 2), BF16),
            pltpu.VMEM((2, SIDE, 4, 16, DA // 2), BF16),
            pltpu.VMEM((2, 4, SIDE, 32, COLS), BF16),
            pltpu.VMEM((2, SIDE, 4, 32, COLS), BF16),
            dma((9,)),
            dma((3, 7)),
            dma((3, 8)),
            dma,
            dma((8,)),
            dma((4,)),
            dma((4,)),
            dma((4, 3)),
            dma((4, 3)),
            dma((4, 3)),
            dma((4, 4)),
        ],
        compiler_params=pltpu.CompilerParams(
            collective_id=0, has_side_effects=True, vmem_limit_bytes=48 * 1024 * 1024
        ),
    )(edge_counts, *(pltpu.with_memory_space_constraint(a, pltpu.HBM) for a in inputs))
    results = (updated, grad_atoms, out2, out1.reshape(DE, DA))
    return pl.pallas_call(
        place,
        out_shape=tuple(jax.ShapeDtypeStruct(a.shape, a.dtype) for a in results),
        in_specs=[vmem] * 4,
        out_specs=(hbm,) * 4,
        scratch_shapes=[dma((18,))],
    )(*(pltpu.with_memory_space_constraint(a, pltpu.VMEM) for a in results))


def solution(mesh):
    rows = P("dp", "graph", None)
    flat = P("dp", "graph")
    return jax.shard_map(
        local,
        mesh=mesh,
        in_specs=(rows, rows, flat, flat, rows, flat, flat, P(), P(), P()),
        out_specs=(rows, rows, P(), P()),
        check_vma=False,
    )
```

```python
import math

import jax
import jax.numpy as jnp
from jax import lax
from jax.experimental import pallas as pl
from jax.experimental.pallas import tpu as pltpu
from jax.sharding import PartitionSpec as P

MESH = pl.DeviceIdType.MESH
F32 = jnp.float32
BF16 = jnp.bfloat16

OWN = 24
ATOMS = 192
EDGES = 512
DA = 512
DE = 1024
NR = 128
SLOT = 2 * OWN
PAD = 32
COLS = 128
SIDE = 8
NEAR = (0, 1, 7, 2, 6, 3, 5, 4)
NEAR_X = (0, 1, 3, 2)
GROUPS = ((1, 3), (3, 5), (5, 8))
GROUPS_X = ((1, 3), (3, 4))


def dot(left, right):
    return jnp.dot(left, right, preferred_element_type=F32)


def dot_nt(left, right):
    return lax.dot_general(left, right, (((1,), (1,)), ((), ())), preferred_element_type=F32)


def dot_tn(left, right):
    return lax.dot_general(left, right, (((0,), (0,)), ((), ())), preferred_element_type=F32)


def hot(hit):
    return hit.astype(F32).astype(BF16)


def by_owner(index):
    return (index * 683) >> 14


def body(count_ref, *refs):
    inputs, refs = refs[:9], refs[9:]
    updated_ref, grad_atoms_ref, out1, out2 = refs[:4]
    (
        atoms_ref,
        cot_ref,
        src_ref,
        dst_ref,
        env_ref,
        ow_ref,
        rw_ref,
        sw_ref,
        basis,
        table,
        full,
        atoms_s,
        atoms_t,
        cot_s,
        rows_s,
        back_s,
        hot_src_s,
        hot_dst_s,
        hott_src_s,
        hott_dst_s,
        grow_s,
        weight_s,
        sum_s,
        rows_out,
        rows_in,
        ga,
        gb,
        ra,
        rb,
        pa,
        pb,
        a1,
        a2,
        b1,
        b2,
        load_sem,
        in_send,
        in_recv,
        row_send,
        row_recv,
        sum_send,
        sum_recv,
        g_send,
        near_recv,
        far_recv,
        core_recv,
    ) = refs[4:]
    dp = lax.axis_index("dp")
    g = lax.axis_index("graph")
    y, z = lax.div(dp, SIDE), lax.rem(dp, SIDE)
    x, core = lax.div(g, 2), lax.rem(g, 2)
    other = 1 - core
    scale = math.sqrt(OWN / EDGES)
    me = (dp, g)

    def send(src, dst, send_sem, recv_sem, device):
        pltpu.make_async_remote_copy(
            src_ref=src, dst_ref=dst, send_sem=send_sem, recv_sem=recv_sem, device_id=device, device_id_type=MESH
        ).start()

    def arrived(dst, sem):
        pltpu.make_async_remote_copy(
            src_ref=dst, dst_ref=dst, send_sem=sem, recv_sem=sem, device_id=me, device_id_type=MESH
        ).wait_recv()

    def sent(src, sem):
        pltpu.make_async_remote_copy(
            src_ref=src, dst_ref=src, send_sem=sem, recv_sem=sem, device_id=me, device_id_type=MESH
        ).wait_send()

    y_at = [lax.rem(y + k, SIDE) for k in range(SIDE)]
    z_at = [lax.rem(z + k, SIDE) for k in range(SIDE)]
    x_at = [lax.rem(x + k, 4) for k in range(4)]
    y_peer = [(y_at[k] * SIDE + z, g) for k in range(SIDE)]
    z_peer = [(y * SIDE + z_at[k], g) for k in range(SIDE)]
    x_peer = [(dp, 2 * x_at[k] + core) for k in range(4)]
    x_peer_other = [(dp, 2 * x_at[k] + other) for k in range(4)]
    sibling = x_peer_other[0]
    graph_peers = [x_peer[2], x_peer_other[2], x_peer[1], x_peer_other[1], x_peer[3], x_peer_other[3], sibling]

    barrier = pltpu.get_barrier_semaphore()
    for peer in graph_peers:
        pl.semaphore_signal(barrier, inc=1, device_id=peer, device_id_type=MESH)
    held = (atoms_ref, cot_ref, src_ref, dst_ref, basis.at[g], env_ref, sw_ref, rw_ref, ow_ref)
    loads = []
    for i, ref in enumerate(held):
        source = inputs[i].at[0] if i == 4 else inputs[i]
        loads.append(pltpu.make_async_copy(source, ref, load_sem.at[i]))
    for i in (0, 1, 2, 3, 5, 4, 6, 7, 8):
        loads[i].start()
    for k in reversed(NEAR[1:]):
        for peer in (y_peer[k], z_peer[k]):
            pl.semaphore_signal(barrier, inc=1, device_id=peer, device_id_type=MESH)

    loads[0].wait()
    loads[1].wait()
    full[g] = jnp.concatenate([atoms_ref[0], cot_ref[0]], axis=0)
    for i in (2, 3, 5):
        loads[i].wait()
    slots = lax.broadcasted_iota(jnp.int32, (1, EDGES), 1)
    live = (slots < count_ref[0, 0]).astype(F32)
    lines = (src_ref[...].astype(F32), dst_ref[...].astype(F32), env_ref[...] * live, jnp.zeros((1, EDGES), F32))
    table[g] = jnp.concatenate([line[:, j * 128 : (j + 1) * 128] for line in lines for j in range(4)], axis=0)
    loads[4].wait()
    pl.semaphore_wait(barrier, 21)
    gathered = (full, table, basis)

    def offer(n, k):
        buf = gathered[n]
        send(buf.at[g], buf.at[g], in_send.at[n, k], in_recv.at[n, g], x_peer[k] if k else sibling)

    for n in (1, 0, 2):
        for k in (2, 1, 3, 0):
            if n < 2 or k != 2:
                offer(n, k)

    def block(k, c):
        return 2 * x_at[k] + c

    def relay(n, k):
        b = block(k, core)
        buf = gathered[n]
        arrived(buf.at[b], in_recv.at[n, b])
        send(buf.at[b], buf.at[b], in_send.at[n, 3 + k], in_recv.at[n, b], sibling)

    def select(b):
        lines = table[b]
        columns = lines.T
        row_atom = lax.broadcasted_iota(jnp.int32, (ATOMS, 128), 0).astype(F32)
        col_atom = lax.broadcasted_iota(jnp.int32, (128, ATOMS), 1).astype(F32)
        for j in range(4):
            edges = pl.ds(j * 128, 128)
            hot_src_s[b, edges, :] = hot(col_atom == columns[:, j : j + 1])
            hot_dst_s[b, edges, :] = hot(col_atom == columns[:, 4 + j : 5 + j])
            weight_s[b, edges, :] = jnp.broadcast_to(columns[:, 8 + j : 9 + j], (128, COLS))
            hott_src_s[b, :, edges] = hot(row_atom == lines[j : j + 1, :])
            hott_dst_s[b, :, edges] = hot(row_atom == lines[4 + j : 5 + j, :])

    select(g)
    pick_r = lax.broadcasted_iota(jnp.int32, (ATOMS, 8 * SLOT), 0)
    pick_c = lax.broadcasted_iota(jnp.int32, (ATOMS, 8 * SLOT), 1)
    pick_at = pick_r + OWN * by_owner(pick_r)
    pick_atoms = hot(pick_c == pick_at)
    pick_cot = hot(pick_c == pick_at + OWN)
    grow_r = lax.broadcasted_iota(jnp.int32, (8 * PAD, ATOMS), 0)
    grow_c = lax.broadcasted_iota(jnp.int32, (8 * PAD, ATOMS), 1)
    inner = grow_r & (PAD - 1)
    grow_s[...] = hot((inner < OWN) & (grow_c == (grow_r >> 5) * OWN + inner))
    arrived(table.at[block(0, other)], in_recv.at[1, block(0, other)])
    select(block(0, other))
    offer(2, 2)
    for k in (1, 3, 2):
        relay(1, k)
    for k in (1, 3, 2):
        select(block(k, core))
        relay(0, k)
    for k in (1, 3, 2):
        arrived(table.at[block(k, other)], in_recv.at[1, block(k, other)])
        select(block(k, other))
    for i in (6, 7, 8):
        loads[i].wait()
    for k in range(4):
        arrived(full.at[block(k, other)], in_recv.at[0, block(k, other)])
    both = full[...].reshape(8 * SLOT, DA)
    atoms = dot(pick_atoms, both).astype(BF16)
    cot = dot(pick_cot, both).astype(BF16)
    atoms_s[...] = atoms
    cot_s[...] = cot
    own_cols = pl.ds(pl.multiple_of(g * COLS, COLS), COLS)
    product = dot(atoms, sw_ref[:, own_cols])
    high = product.astype(BF16)
    rows_s[:, :COLS] = high
    rows_s[:, COLS:] = (product - high.astype(F32)).astype(BF16)
    back_s[...] = (dot_nt(cot, ow_ref[own_cols, :]) * scale).astype(BF16)

    def edges_of(b):
        at_src = dot(hot_src_s[b], rows_s[...])
        pre = dot(basis[b], rw_ref[:, own_cols]) + at_src[:, :COLS] + at_src[:, COLS:]
        pulled = dot(hot_dst_s[b], back_s[...])
        weight = weight_s[b]
        sigma = 0.5 * jnp.tanh(0.5 * pre) + 0.5
        silu = pre * sigma
        slope = sigma + silu * (1.0 - sigma)
        message = (silu * weight).astype(BF16)
        dpre = (pulled * weight * slope).astype(BF16)
        return dot(hott_dst_s[b], message), dot(hott_src_s[b], dpre)

    def add(*blocks):
        terms = [edges_of(b) for b in blocks]
        for i in range(2):
            sum_s[i] += sum((term[i] for term in terms[1:]), terms[0][i])

    sum_s[...] = jnp.zeros_like(sum_s)
    arrived(basis.at[block(0, other)], in_recv.at[2, block(0, other)])
    add(g, block(0, other))
    for k in (1, 3):
        relay(2, k)
    add(block(1, core), block(3, core))
    atoms_t[...] = atoms_s[...].astype(F32).T.astype(BF16)
    for k in (1, 3):
        arrived(basis.at[block(k, other)], in_recv.at[2, block(k, other)])
    relay(2, 2)
    add(block(1, other), block(3, other), block(2, core))
    arrived(basis.at[block(2, other)], in_recv.at[2, block(2, other)])
    add(block(2, other))
    sums = sum_s[...].astype(BF16)
    summed, dsum = sums[0], sums[1]

    ga[...] = dot(sum_s[0].T.astype(BF16), cot_s[...]).astype(BF16).reshape(SIDE, 16, DA)
    for k in reversed(NEAR[1:]):
        send(ga.at[y_at[k]], ra.at[k], sum_send.at[0], sum_recv.at[0], y_peer[k])
    gb[...] = dot(atoms_t[...], dsum).astype(BF16).reshape(SIDE, 64, COLS)
    for k in reversed(NEAR[1:]):
        send(gb.at[z_at[k]], rb.at[k], sum_send.at[1], sum_recv.at[1], z_peer[k])

    rows_out[:, 0] = dot(grow_s[...], summed).astype(BF16).reshape(8, PAD, COLS)
    rows_out[:, 1] = dot(grow_s[...], dsum).astype(BF16).reshape(8, PAD, COLS)
    rows_in[:, :, own_cols] = rows_out[g]
    for peer in graph_peers:
        send(rows_out.at[peer[1]], rows_in.at[:, :, own_cols], row_send, row_recv.at[g], peer)

    def total(own, parts):
        acc = own.astype(F32)
        for k in range(1, SIDE):
            acc = acc + parts[k].astype(F32)
        return acc.astype(BF16)

    arrived(ra.at[pl.ds(1, 7)], sum_recv.at[0])
    pa[0] = total(ga[y], ra)
    for k in reversed(NEAR[1:]):
        send(pa.at[0], pa.at[k], sum_send.at[2], sum_recv.at[2], z_peer[k])
    arrived(rb.at[pl.ds(1, 7)], sum_recv.at[1])
    pb[0] = total(gb[z], rb)
    for k in reversed(NEAR[1:]):
        send(pb.at[0], pb.at[k], sum_send.at[3], sum_recv.at[3], y_peer[k])

    for peer in graph_peers:
        peer_cols = pl.ds(pl.multiple_of(peer[1] * COLS, COLS), COLS)
        arrived(rows_in.at[:, :, peer_cols], row_recv.at[peer[1]])
    update = dot(rows_in[0], ow_ref[...]) * scale
    updated_ref[0] = (atoms_ref[0].astype(F32) + update[:OWN]).astype(BF16)
    pushed = dot_nt(rows_in[1], sw_ref[...])
    grad_atoms_ref[0] = (cot_ref[0].astype(F32) + pushed[:OWN]).astype(BF16)

    def settle(at, parts, factor):
        acc = parts[at].astype(F32)
        for j in range(1, SIDE):
            acc = acc + parts[lax.rem(at + SIDE - j, SIDE)].astype(F32)
        return (acc * factor).astype(BF16)

    systems = SIDE * SIDE

    back_to = [[y_peer[(SIDE - k) % SIDE] for k in NEAR], [z_peer[(SIDE - k) % SIDE] for k in NEAR]]
    back_x = [x_peer[(4 - k) % 4] for k in NEAR_X]
    first = ((a1, 0, back_to[0]), (b1, 1, back_to[1]))
    second = ((a2, 2, back_to[0]), (b2, 3, back_to[1]))

    def group_of(s):
        return 0 if s < 3 else 1 if s < 5 else 2

    def pass_first(buf, n, lo, hi):
        for s in (3, 1, 2):
            send(
                buf.at[core, 0, pl.ds(lo, hi - lo)],
                buf.at[core, s, pl.ds(lo, hi - lo)],
                g_send.at[n, 1],
                far_recv.at[n, s - 1],
                back_x[s],
            )

    def pass_second(buf, n, peers, lo, hi):
        for s in range(7, 0, -1):
            send(
                buf.at[core, 0, pl.ds(lo, hi - lo)],
                buf.at[core, s, pl.ds(lo, hi - lo)],
                g_send.at[n, 1],
                far_recv.at[n, group_of(s)],
                peers[s],
            )

    def pass_core(buf, n, slot, lo, hi):
        send(
            buf.at[core, pl.ds(lo, hi - lo)],
            buf.at[core, pl.ds(lo, hi - lo)],
            g_send.at[n, 2],
            core_recv.at[n, slot],
            sibling,
        )

    for turn in range(2):
        if turn == 0:
            arrived(pa.at[pl.ds(1, 7)], sum_recv.at[2])
            piece = settle(z, pa, scale / math.sqrt(systems * ATOMS))
            a1[core, 0, 0] = piece[:, : DA // 2]
            a2[core, 0, 0] = piece[:, DA // 2 :]
        else:
            arrived(pb.at[pl.ds(1, 7)], sum_recv.at[3])
            piece = settle(y, pb, 16.0 / math.sqrt(systems * 8 * EDGES))
            b1[core, 0, 0] = piece[:32]
            b2[core, 0, 0] = piece[32:]
        buf, n, peers = second[turn]
        for s in (3, 1, 2):
            send(buf.at[core, 0, 0], buf.at[core, 0, s], g_send.at[n, 0], near_recv.at[n, 0 if s < 3 else 1], back_x[s])
        buf, n, peers = first[turn]
        for s in range(7, 0, -1):
            send(buf.at[core, 0, 0], buf.at[core, 0, s], g_send.at[n, 0], near_recv.at[n, group_of(s)], peers[s])
        pass_first(buf, n, 0, 1)
    for buf, n, peers in second:
        pass_second(buf, n, peers, 0, 1)
    for i in range(3):
        if i < 2:
            lo, hi = GROUPS_X[i]
            for buf, n, peers in second:
                arrived(buf.at[core, 0, pl.ds(lo, hi - lo)], near_recv.at[n, i])
                pass_second(buf, n, peers, lo, hi)
        lo, hi = GROUPS[i]
        for buf, n, peers in first:
            arrived(buf.at[core, 0, pl.ds(lo, hi - lo)], near_recv.at[n, i])
            pass_first(buf, n, lo, hi)
    for buf, n, peers in second + first:
        pass_core(buf, n, 0, 0, 1)

    def store(n, c, xs, ys):
        owner = 2 * x_at[NEAR_X[xs]] + c
        if n in (0, 2):
            piece = a1[c, xs, ys] if n == 0 else a2[c, ys, xs]
            half = slice(0, DA // 2) if n == 0 else slice(DA // 2, DA)
            out1[owner, y_at[NEAR[ys]], :, half] = piece
        else:
            piece = b1[c, xs, ys] if n == 1 else b2[c, ys, xs]
            rows = pl.ds(pl.multiple_of(z_at[NEAR[ys]] * 64 + (0 if n == 1 else 32), 32), 32)
            out2[rows, pl.ds(pl.multiple_of(owner * COLS, COLS), COLS)] = piece

    def store_all(n, c, lo, hi):
        for s in range(lo, hi):
            for t in range(8 if n < 2 else 4):
                if n < 2:
                    store(n, c, s, t)
                else:
                    store(n, c, t, s)

    for buf, n, peers in second + first:
        store_all(n, core, 0, 1)
    parts = []
    for i in range(3):
        for buf, n, peers in second:
            parts.append((buf, n, i, *GROUPS[i]))
        for buf, n, peers in first:
            parts.append((buf, n, i, i + 1, i + 2))
    for buf, n, i, lo, hi in parts:
        arrived(buf.at[core, pl.ds(lo, hi - lo)], far_recv.at[n, i])
        pass_core(buf, n, i + 1, lo, hi)
        store_all(n, core, lo, hi)
    for buf, n, peers in second + first:
        arrived(buf.at[other, pl.ds(0, 1)], core_recv.at[n, 0])
        store_all(n, other, 0, 1)
    for buf, n, i, lo, hi in parts:
        arrived(buf.at[other, pl.ds(lo, hi - lo)], core_recv.at[n, i + 1])
        store_all(n, other, lo, hi)

    for buf, n, peers in first + second:
        sent(buf.at[core, 0, pl.ds(1, 7 if n < 2 else 3)], g_send.at[n, 0])
        sent(buf.at[core, pl.ds(1, 3 if n < 2 else 7)], g_send.at[n, 1])
        sent(buf.at[core], g_send.at[n, 2])
    for n, buf in enumerate(gathered):
        for k in range(7):
            sent(buf.at[0], in_send.at[n, k])
    sent(rows_out.at[pl.ds(0, 7)], row_send)
    sent(ra.at[pl.ds(1, 7)], sum_send.at[0])
    sent(rb.at[pl.ds(1, 7)], sum_send.at[1])
    sent(pa.at[pl.ds(1, 7)], sum_send.at[2])
    sent(pb.at[pl.ds(1, 7)], sum_send.at[3])


def place(*refs):
    sems = refs[8]
    copies = [pltpu.make_async_copy(refs[i], refs[4 + i], sems.at[i]) for i in range(2)]
    for i in (2, 3):
        rows = refs[i].shape[0] // 8
        for j in range(8):
            part = pl.ds(j * rows, rows)
            copies.append(pltpu.make_async_copy(refs[i].at[part], refs[4 + i].at[part], sems.at[len(copies)]))
    for c in copies:
        c.start()
    for c in copies:
        c.wait()


def local(atoms, cotangent, sources, targets, radial, envelope, edge_counts, source_weight, radial_weight, output_weight):
    inputs = (atoms, cotangent, sources, targets, radial, envelope, source_weight, radial_weight, output_weight)
    vmem = pl.BlockSpec(memory_space=pltpu.VMEM)
    hbm = pl.BlockSpec(memory_space=pltpu.HBM)
    smem = pl.BlockSpec(memory_space=pltpu.SMEM)
    dma = pltpu.SemaphoreType.DMA

    def like(a):
        return pltpu.VMEM(a.shape, a.dtype)

    updated, grad_atoms, out1, out2 = pl.pallas_call(
        body,
        out_shape=(
            pltpu.VMEM((1, OWN, DA), BF16),
            pltpu.VMEM((1, OWN, DA), BF16),
            pltpu.VMEM((8, SIDE, 16, DA), BF16),
            pltpu.VMEM((DA, DE), BF16),
        ),
        in_specs=[smem] + [hbm] * 9,
        out_specs=(vmem,) * 4,
        scratch_shapes=[
            like(atoms),
            like(cotangent),
            like(sources),
            like(targets),
            like(envelope),
            like(output_weight),
            like(radial_weight),
            like(source_weight),
            pltpu.VMEM((8, EDGES, NR), BF16),
            pltpu.VMEM((8, 16, 128), F32),
            pltpu.VMEM((8, SLOT, DA), BF16),
            pltpu.VMEM((ATOMS, DA), BF16),
            pltpu.VMEM((DA, ATOMS), BF16),
            pltpu.VMEM((ATOMS, DA), BF16),
            pltpu.VMEM((ATOMS, 2 * COLS), BF16),
            pltpu.VMEM((ATOMS, COLS), BF16),
            pltpu.VMEM((8, EDGES, ATOMS), BF16),
            pltpu.VMEM((8, EDGES, ATOMS), BF16),
            pltpu.VMEM((8, ATOMS, EDGES), BF16),
            pltpu.VMEM((8, ATOMS, EDGES), BF16),
            pltpu.VMEM((8 * PAD, ATOMS), BF16),
            pltpu.VMEM((8, EDGES, COLS), F32),
            pltpu.VMEM((2, ATOMS, COLS), F32),
            pltpu.VMEM((8, 2, PAD, COLS), BF16),
            pltpu.VMEM((2, PAD, DE), BF16),
            pltpu.VMEM((SIDE, 16, DA), BF16),
            pltpu.VMEM((SIDE, 64, COLS), BF16),
            pltpu.VMEM((SIDE, 16, DA), BF16),
            pltpu.VMEM((SIDE, 64, COLS), BF16),
            pltpu.VMEM((SIDE, 16, DA), BF16),
            pltpu.VMEM((SIDE, 64, COLS), BF16),
            pltpu.VMEM((2, 4, SIDE, 16, DA // 2), BF16),
            pltpu.VMEM((2, SIDE, 4, 16, DA // 2), BF16),
            pltpu.VMEM((2, 4, SIDE, 32, COLS), BF16),
            pltpu.VMEM((2, SIDE, 4, 32, COLS), BF16),
            dma((9,)),
            dma((3, 7)),
            dma((3, 8)),
            dma,
            dma((8,)),
            dma((4,)),
            dma((4,)),
            dma((4, 3)),
            dma((4, 3)),
            dma((4, 3)),
            dma((4, 4)),
        ],
        compiler_params=pltpu.CompilerParams(
            collective_id=0, has_side_effects=True, vmem_limit_bytes=48 * 1024 * 1024
        ),
    )(edge_counts, *(pltpu.with_memory_space_constraint(a, pltpu.HBM) for a in inputs))
    results = (updated, grad_atoms, out2, out1.reshape(DE, DA))
    return pl.pallas_call(
        place,
        out_shape=tuple(jax.ShapeDtypeStruct(a.shape, a.dtype) for a in results),
        in_specs=[vmem] * 4,
        out_specs=(hbm,) * 4,
        scratch_shapes=[dma((18,))],
    )(*(pltpu.with_memory_space_constraint(a, pltpu.VMEM) for a in results))


def solution(mesh):
    rows = P("dp", "graph", None)
    flat = P("dp", "graph")
    return jax.shard_map(
        local,
        mesh=mesh,
        in_specs=(rows, rows, flat, flat, rows, flat, flat, P(), P(), P()),
        out_specs=(rows, rows, P(), P()),
        check_vma=False,
    )
```

```python
import math

import jax
import jax.numpy as jnp
from jax import lax
from jax.experimental import pallas as pl
from jax.experimental.pallas import tpu as pltpu
from jax.sharding import PartitionSpec as P

MESH = pl.DeviceIdType.MESH
F32 = jnp.float32
BF16 = jnp.bfloat16

OWN = 24
ATOMS = 192
EDGES = 512
DA = 512
DE = 1024
NR = 128
SLOT = 2 * OWN
PAD = 32
COLS = 128
SIDE = 8
NEAR = (0, 1, 7, 2, 6, 3, 5, 4)
NEAR_X = (0, 1, 3, 2)
GROUPS = ((1, 3), (3, 5), (5, 8))
GROUPS_X = ((1, 3), (3, 4))


def dot(left, right):
    return jnp.dot(left, right, preferred_element_type=F32)


def dot_nt(left, right):
    return lax.dot_general(left, right, (((1,), (1,)), ((), ())), preferred_element_type=F32)


def dot_tn(left, right):
    return lax.dot_general(left, right, (((0,), (0,)), ((), ())), preferred_element_type=F32)


def hot(hit):
    return hit.astype(F32).astype(BF16)


def by_owner(index):
    return (index * 683) >> 14


def body(count_ref, *refs):
    inputs, refs = refs[:9], refs[9:]
    updated_ref, grad_atoms_ref, out1, out2 = refs[:4]
    (
        atoms_ref,
        cot_ref,
        src_ref,
        dst_ref,
        env_ref,
        ow_ref,
        rw_ref,
        sw_ref,
        basis,
        table,
        full,
        atoms_s,
        atoms_t,
        cot_s,
        rows_s,
        back_s,
        hot_src_s,
        hot_dst_s,
        hott_src_s,
        hott_dst_s,
        grow_s,
        weight_s,
        sum_s,
        rows_out,
        rows_in,
        ga,
        gb,
        ra,
        rb,
        pa,
        pb,
        a1,
        a2,
        b1,
        b2,
        load_sem,
        in_send,
        in_recv,
        row_send,
        row_recv,
        sum_send,
        sum_recv,
        g_send,
        near_recv,
        far_recv,
        core_recv,
    ) = refs[4:]
    dp = lax.axis_index("dp")
    g = lax.axis_index("graph")
    y, z = lax.div(dp, SIDE), lax.rem(dp, SIDE)
    x, core = lax.div(g, 2), lax.rem(g, 2)
    other = 1 - core
    scale = math.sqrt(OWN / EDGES)
    me = (dp, g)

    def send(src, dst, send_sem, recv_sem, device):
        pltpu.make_async_remote_copy(
            src_ref=src, dst_ref=dst, send_sem=send_sem, recv_sem=recv_sem, device_id=device, device_id_type=MESH
        ).start()

    def arrived(dst, sem):
        pltpu.make_async_remote_copy(
            src_ref=dst, dst_ref=dst, send_sem=sem, recv_sem=sem, device_id=me, device_id_type=MESH
        ).wait_recv()

    def sent(src, sem):
        pltpu.make_async_remote_copy(
            src_ref=src, dst_ref=src, send_sem=sem, recv_sem=sem, device_id=me, device_id_type=MESH
        ).wait_send()

    y_at = [lax.rem(y + k, SIDE) for k in range(SIDE)]
    z_at = [lax.rem(z + k, SIDE) for k in range(SIDE)]
    x_at = [lax.rem(x + k, 4) for k in range(4)]
    y_peer = [(y_at[k] * SIDE + z, g) for k in range(SIDE)]
    z_peer = [(y * SIDE + z_at[k], g) for k in range(SIDE)]
    x_peer = [(dp, 2 * x_at[k] + core) for k in range(4)]
    x_peer_other = [(dp, 2 * x_at[k] + other) for k in range(4)]
    sibling = x_peer_other[0]
    graph_peers = [x_peer[2], x_peer_other[2], x_peer[1], x_peer_other[1], x_peer[3], x_peer_other[3], sibling]

    barrier = pltpu.get_barrier_semaphore()
    for peer in graph_peers:
        pl.semaphore_signal(barrier, inc=1, device_id=peer, device_id_type=MESH)
    held = (atoms_ref, cot_ref, src_ref, dst_ref, basis.at[g], env_ref, sw_ref, rw_ref, ow_ref)
    loads = []
    for i, ref in enumerate(held):
        source = inputs[i].at[0] if i == 4 else inputs[i]
        loads.append(pltpu.make_async_copy(source, ref, load_sem.at[i]))
    for i in (0, 1, 2, 3, 5, 4, 6, 7, 8):
        loads[i].start()
    for k in reversed(NEAR[1:]):
        for peer in (y_peer[k], z_peer[k]):
            pl.semaphore_signal(barrier, inc=1, device_id=peer, device_id_type=MESH)

    loads[0].wait()
    loads[1].wait()
    full[g] = jnp.concatenate([atoms_ref[0], cot_ref[0]], axis=0)
    for i in (2, 3, 5):
        loads[i].wait()
    slots = lax.broadcasted_iota(jnp.int32, (1, EDGES), 1)
    live = (slots < count_ref[0, 0]).astype(F32)
    lines = (src_ref[...].astype(F32), dst_ref[...].astype(F32), env_ref[...] * live, jnp.zeros((1, EDGES), F32))
    table[g] = jnp.concatenate([line[:, j * 128 : (j + 1) * 128] for line in lines for j in range(4)], axis=0)
    loads[4].wait()
    pl.semaphore_wait(barrier, 21)
    gathered = (full, table, basis)

    def offer(n, k):
        buf = gathered[n]
        send(buf.at[g], buf.at[g], in_send.at[n, k], in_recv.at[n, g], x_peer[k] if k else sibling)

    for n in (1, 0, 2):
        for k in (2, 1, 3, 0):
            if n < 2 or k != 2:
                offer(n, k)

    def block(k, c):
        return 2 * x_at[k] + c

    def relay(n, k):
        b = block(k, core)
        buf = gathered[n]
        arrived(buf.at[b], in_recv.at[n, b])
        send(buf.at[b], buf.at[b], in_send.at[n, 3 + k], in_recv.at[n, b], sibling)

    def select(b):
        lines = table[b]
        columns = lines.T
        row_atom = lax.broadcasted_iota(jnp.int32, (ATOMS, 128), 0).astype(F32)
        col_atom = lax.broadcasted_iota(jnp.int32, (128, ATOMS), 1).astype(F32)
        for j in range(4):
            edges = pl.ds(j * 128, 128)
            hot_src_s[b, edges, :] = hot(col_atom == columns[:, j : j + 1])
            hot_dst_s[b, edges, :] = hot(col_atom == columns[:, 4 + j : 5 + j])
            weight_s[b, edges, :] = jnp.broadcast_to(columns[:, 8 + j : 9 + j], (128, COLS))
            hott_src_s[b, :, edges] = hot(row_atom == lines[j : j + 1, :])
            hott_dst_s[b, :, edges] = hot(row_atom == lines[4 + j : 5 + j, :])

    select(g)
    pick_r = lax.broadcasted_iota(jnp.int32, (ATOMS, 8 * SLOT), 0)
    pick_c = lax.broadcasted_iota(jnp.int32, (ATOMS, 8 * SLOT), 1)
    pick_at = pick_r + OWN * by_owner(pick_r)
    pick_atoms = hot(pick_c == pick_at)
    pick_cot = hot(pick_c == pick_at + OWN)
    grow_r = lax.broadcasted_iota(jnp.int32, (8 * PAD, ATOMS), 0)
    grow_c = lax.broadcasted_iota(jnp.int32, (8 * PAD, ATOMS), 1)
    inner = grow_r & (PAD - 1)
    grow_s[...] = hot((inner < OWN) & (grow_c == (grow_r >> 5) * OWN + inner))
    arrived(table.at[block(0, other)], in_recv.at[1, block(0, other)])
    select(block(0, other))
    offer(2, 2)
    for k in (1, 3, 2):
        relay(1, k)
    for k in (1, 3, 2):
        select(block(k, core))
        relay(0, k)
    for k in (1, 3, 2):
        arrived(table.at[block(k, other)], in_recv.at[1, block(k, other)])
        select(block(k, other))
    for i in (6, 7, 8):
        loads[i].wait()
    for k in range(4):
        arrived(full.at[block(k, other)], in_recv.at[0, block(k, other)])
    both = full[...].reshape(8 * SLOT, DA)
    atoms = dot(pick_atoms, both).astype(BF16)
    cot = dot(pick_cot, both).astype(BF16)
    atoms_s[...] = atoms
    cot_s[...] = cot
    own_cols = pl.ds(pl.multiple_of(g * COLS, COLS), COLS)
    product = dot(atoms, sw_ref[:, own_cols])
    high = product.astype(BF16)
    rows_s[:, :COLS] = high
    rows_s[:, COLS:] = (product - high.astype(F32)).astype(BF16)
    back_s[...] = (dot_nt(cot, ow_ref[own_cols, :]) * scale).astype(BF16)

    def edges_of(b):
        at_src = dot(hot_src_s[b], rows_s[...])
        pre = dot(basis[b], rw_ref[:, own_cols]) + at_src[:, :COLS] + at_src[:, COLS:]
        pulled = dot(hot_dst_s[b], back_s[...])
        weight = weight_s[b]
        sigma = 0.5 * jnp.tanh(0.5 * pre) + 0.5
        silu = pre * sigma
        slope = sigma + silu * (1.0 - sigma)
        message = (silu * weight).astype(BF16)
        dpre = (pulled * weight * slope).astype(BF16)
        return dot(hott_dst_s[b], message), dot(hott_src_s[b], dpre)

    def terms_of(*blocks):
        terms = [edges_of(b) for b in blocks]
        return [sum((term[i] for term in terms[1:]), terms[0][i]) for i in range(2)]

    def add(*blocks):
        terms = terms_of(*blocks)
        for i in range(2):
            sum_s[i] += terms[i]

    arrived(basis.at[block(0, other)], in_recv.at[2, block(0, other)])
    sum_s[0], sum_s[1] = terms_of(g, block(0, other))
    for k in (1, 3):
        relay(2, k)
    add(block(1, core), block(3, core))
    atoms_t[...] = atoms_s[...].astype(F32).T.astype(BF16)
    for k in (1, 3):
        arrived(basis.at[block(k, other)], in_recv.at[2, block(k, other)])
    relay(2, 2)
    add(block(1, other), block(3, other), block(2, core))
    arrived(basis.at[block(2, other)], in_recv.at[2, block(2, other)])
    last = terms_of(block(2, other))
    first_sum = sum_s[0] + last[0]
    summed, dsum = first_sum.astype(BF16), (sum_s[1] + last[1]).astype(BF16)

    ga[...] = dot(first_sum.T.astype(BF16), cot_s[...]).astype(BF16).reshape(SIDE, 16, DA)
    for k in reversed(NEAR[1:]):
        send(ga.at[y_at[k]], ra.at[k], sum_send.at[0], sum_recv.at[0], y_peer[k])
    gb[...] = dot(atoms_t[...], dsum).astype(BF16).reshape(SIDE, 64, COLS)
    for k in reversed(NEAR[1:]):
        send(gb.at[z_at[k]], rb.at[k], sum_send.at[1], sum_recv.at[1], z_peer[k])

    rows_out[:, 0] = dot(grow_s[...], summed).astype(BF16).reshape(8, PAD, COLS)
    rows_out[:, 1] = dot(grow_s[...], dsum).astype(BF16).reshape(8, PAD, COLS)
    rows_in[:, :, own_cols] = rows_out[g]
    for peer in graph_peers:
        send(rows_out.at[peer[1]], rows_in.at[:, :, own_cols], row_send, row_recv.at[g], peer)

    def total(own, parts):
        acc = own.astype(F32)
        for k in range(1, SIDE):
            acc = acc + parts[k].astype(F32)
        return acc.astype(BF16)

    arrived(ra.at[pl.ds(1, 7)], sum_recv.at[0])
    pa[0] = total(ga[y], ra)
    for k in reversed(NEAR[1:]):
        send(pa.at[0], pa.at[k], sum_send.at[2], sum_recv.at[2], z_peer[k])
    arrived(rb.at[pl.ds(1, 7)], sum_recv.at[1])
    pb[0] = total(gb[z], rb)
    for k in reversed(NEAR[1:]):
        send(pb.at[0], pb.at[k], sum_send.at[3], sum_recv.at[3], y_peer[k])

    for peer in graph_peers:
        peer_cols = pl.ds(pl.multiple_of(peer[1] * COLS, COLS), COLS)
        arrived(rows_in.at[:, :, peer_cols], row_recv.at[peer[1]])
    update = dot(rows_in[0], ow_ref[...]) * scale
    updated_ref[0] = (atoms_ref[0].astype(F32) + update[:OWN]).astype(BF16)
    pushed = dot_nt(rows_in[1], sw_ref[...])
    grad_atoms_ref[0] = (cot_ref[0].astype(F32) + pushed[:OWN]).astype(BF16)

    def settle(at, parts, factor):
        acc = parts[at].astype(F32)
        for j in range(1, SIDE):
            acc = acc + parts[lax.rem(at + SIDE - j, SIDE)].astype(F32)
        return (acc * factor).astype(BF16)

    systems = SIDE * SIDE

    back_to = [[y_peer[(SIDE - k) % SIDE] for k in NEAR], [z_peer[(SIDE - k) % SIDE] for k in NEAR]]
    back_x = [x_peer[(4 - k) % 4] for k in NEAR_X]
    first = ((a1, 0, back_to[0]), (b1, 1, back_to[1]))
    second = ((a2, 2, back_to[0]), (b2, 3, back_to[1]))

    def group_of(s):
        return 0 if s < 3 else 1 if s < 5 else 2

    def pass_first(buf, n, lo, hi):
        for s in (3, 1, 2):
            send(
                buf.at[core, 0, pl.ds(lo, hi - lo)],
                buf.at[core, s, pl.ds(lo, hi - lo)],
                g_send.at[n, 1],
                far_recv.at[n, s - 1],
                back_x[s],
            )

    def pass_second(buf, n, peers, lo, hi):
        for s in range(7, 0, -1):
            send(
                buf.at[core, 0, pl.ds(lo, hi - lo)],
                buf.at[core, s, pl.ds(lo, hi - lo)],
                g_send.at[n, 1],
                far_recv.at[n, group_of(s)],
                peers[s],
            )

    def pass_core(buf, n, slot, lo, hi):
        send(
            buf.at[core, pl.ds(lo, hi - lo)],
            buf.at[core, pl.ds(lo, hi - lo)],
            g_send.at[n, 2],
            core_recv.at[n, slot],
            sibling,
        )

    for turn in range(2):
        if turn == 0:
            arrived(pa.at[pl.ds(1, 7)], sum_recv.at[2])
            piece = settle(z, pa, scale / math.sqrt(systems * ATOMS))
            a1[core, 0, 0] = piece[:, : DA // 2]
            a2[core, 0, 0] = piece[:, DA // 2 :]
        else:
            arrived(pb.at[pl.ds(1, 7)], sum_recv.at[3])
            piece = settle(y, pb, 16.0 / math.sqrt(systems * 8 * EDGES))
            b1[core, 0, 0] = piece[:32]
            b2[core, 0, 0] = piece[32:]
        buf, n, peers = second[turn]
        for s in (3, 1, 2):
            send(buf.at[core, 0, 0], buf.at[core, 0, s], g_send.at[n, 0], near_recv.at[n, 0 if s < 3 else 1], back_x[s])
        buf, n, peers = first[turn]
        for s in range(7, 0, -1):
            send(buf.at[core, 0, 0], buf.at[core, 0, s], g_send.at[n, 0], near_recv.at[n, group_of(s)], peers[s])
        pass_first(buf, n, 0, 1)
    for buf, n, peers in second:
        pass_second(buf, n, peers, 0, 1)
    for i in range(3):
        if i < 2:
            lo, hi = GROUPS_X[i]
            for buf, n, peers in second:
                arrived(buf.at[core, 0, pl.ds(lo, hi - lo)], near_recv.at[n, i])
                pass_second(buf, n, peers, lo, hi)
        lo, hi = GROUPS[i]
        for buf, n, peers in first:
            arrived(buf.at[core, 0, pl.ds(lo, hi - lo)], near_recv.at[n, i])
            pass_first(buf, n, lo, hi)
    for buf, n, peers in second + first:
        pass_core(buf, n, 0, 0, 1)

    def store(n, c, xs, ys):
        owner = 2 * x_at[NEAR_X[xs]] + c
        if n in (0, 2):
            piece = a1[c, xs, ys] if n == 0 else a2[c, ys, xs]
            half = slice(0, DA // 2) if n == 0 else slice(DA // 2, DA)
            out1[owner, y_at[NEAR[ys]], :, half] = piece
        else:
            piece = b1[c, xs, ys] if n == 1 else b2[c, ys, xs]
            rows = pl.ds(pl.multiple_of(z_at[NEAR[ys]] * 64 + (0 if n == 1 else 32), 32), 32)
            out2[rows, pl.ds(pl.multiple_of(owner * COLS, COLS), COLS)] = piece

    def store_all(n, c, lo, hi):
        for s in range(lo, hi):
            for t in range(8 if n < 2 else 4):
                if n < 2:
                    store(n, c, s, t)
                else:
                    store(n, c, t, s)

    for buf, n, peers in second + first:
        store_all(n, core, 0, 1)
    parts = []
    for i in range(3):
        for buf, n, peers in second:
            parts.append((buf, n, i, *GROUPS[i]))
        for buf, n, peers in first:
            parts.append((buf, n, i, i + 1, i + 2))
    for buf, n, i, lo, hi in parts:
        arrived(buf.at[core, pl.ds(lo, hi - lo)], far_recv.at[n, i])
        pass_core(buf, n, i + 1, lo, hi)
        store_all(n, core, lo, hi)
    for buf, n, peers in second + first:
        arrived(buf.at[other, pl.ds(0, 1)], core_recv.at[n, 0])
        store_all(n, other, 0, 1)
    for buf, n, i, lo, hi in parts:
        arrived(buf.at[other, pl.ds(lo, hi - lo)], core_recv.at[n, i + 1])
        store_all(n, other, lo, hi)

    for buf, n, peers in first + second:
        sent(buf.at[core, 0, pl.ds(1, 7 if n < 2 else 3)], g_send.at[n, 0])
        sent(buf.at[core, pl.ds(1, 3 if n < 2 else 7)], g_send.at[n, 1])
        sent(buf.at[core], g_send.at[n, 2])
    for n, buf in enumerate(gathered):
        for k in range(7):
            sent(buf.at[0], in_send.at[n, k])
    sent(rows_out.at[pl.ds(0, 7)], row_send)
    sent(ra.at[pl.ds(1, 7)], sum_send.at[0])
    sent(rb.at[pl.ds(1, 7)], sum_send.at[1])
    sent(pa.at[pl.ds(1, 7)], sum_send.at[2])
    sent(pb.at[pl.ds(1, 7)], sum_send.at[3])


def place(*refs):
    sems = refs[8]
    copies = [pltpu.make_async_copy(refs[i], refs[4 + i], sems.at[i]) for i in range(2)]
    for i in (2, 3):
        rows = refs[i].shape[0] // 8
        for j in range(8):
            part = pl.ds(j * rows, rows)
            copies.append(pltpu.make_async_copy(refs[i].at[part], refs[4 + i].at[part], sems.at[len(copies)]))
    for c in copies:
        c.start()
    for c in copies:
        c.wait()


def local(atoms, cotangent, sources, targets, radial, envelope, edge_counts, source_weight, radial_weight, output_weight):
    inputs = (atoms, cotangent, sources, targets, radial, envelope, source_weight, radial_weight, output_weight)
    vmem = pl.BlockSpec(memory_space=pltpu.VMEM)
    hbm = pl.BlockSpec(memory_space=pltpu.HBM)
    smem = pl.BlockSpec(memory_space=pltpu.SMEM)
    dma = pltpu.SemaphoreType.DMA

    def like(a):
        return pltpu.VMEM(a.shape, a.dtype)

    updated, grad_atoms, out1, out2 = pl.pallas_call(
        body,
        out_shape=(
            pltpu.VMEM((1, OWN, DA), BF16),
            pltpu.VMEM((1, OWN, DA), BF16),
            pltpu.VMEM((8, SIDE, 16, DA), BF16),
            pltpu.VMEM((DA, DE), BF16),
        ),
        in_specs=[smem] + [hbm] * 9,
        out_specs=(vmem,) * 4,
        scratch_shapes=[
            like(atoms),
            like(cotangent),
            like(sources),
            like(targets),
            like(envelope),
            like(output_weight),
            like(radial_weight),
            like(source_weight),
            pltpu.VMEM((8, EDGES, NR), BF16),
            pltpu.VMEM((8, 16, 128), F32),
            pltpu.VMEM((8, SLOT, DA), BF16),
            pltpu.VMEM((ATOMS, DA), BF16),
            pltpu.VMEM((DA, ATOMS), BF16),
            pltpu.VMEM((ATOMS, DA), BF16),
            pltpu.VMEM((ATOMS, 2 * COLS), BF16),
            pltpu.VMEM((ATOMS, COLS), BF16),
            pltpu.VMEM((8, EDGES, ATOMS), BF16),
            pltpu.VMEM((8, EDGES, ATOMS), BF16),
            pltpu.VMEM((8, ATOMS, EDGES), BF16),
            pltpu.VMEM((8, ATOMS, EDGES), BF16),
            pltpu.VMEM((8 * PAD, ATOMS), BF16),
            pltpu.VMEM((8, EDGES, COLS), F32),
            pltpu.VMEM((2, ATOMS, COLS), F32),
            pltpu.VMEM((8, 2, PAD, COLS), BF16),
            pltpu.VMEM((2, PAD, DE), BF16),
            pltpu.VMEM((SIDE, 16, DA), BF16),
            pltpu.VMEM((SIDE, 64, COLS), BF16),
            pltpu.VMEM((SIDE, 16, DA), BF16),
            pltpu.VMEM((SIDE, 64, COLS), BF16),
            pltpu.VMEM((SIDE, 16, DA), BF16),
            pltpu.VMEM((SIDE, 64, COLS), BF16),
            pltpu.VMEM((2, 4, SIDE, 16, DA // 2), BF16),
            pltpu.VMEM((2, SIDE, 4, 16, DA // 2), BF16),
            pltpu.VMEM((2, 4, SIDE, 32, COLS), BF16),
            pltpu.VMEM((2, SIDE, 4, 32, COLS), BF16),
            dma((9,)),
            dma((3, 7)),
            dma((3, 8)),
            dma,
            dma((8,)),
            dma((4,)),
            dma((4,)),
            dma((4, 3)),
            dma((4, 3)),
            dma((4, 3)),
            dma((4, 4)),
        ],
        compiler_params=pltpu.CompilerParams(
            collective_id=0, has_side_effects=True, vmem_limit_bytes=48 * 1024 * 1024
        ),
    )(edge_counts, *(pltpu.with_memory_space_constraint(a, pltpu.HBM) for a in inputs))
    results = (updated, grad_atoms, out2, out1.reshape(DE, DA))
    return pl.pallas_call(
        place,
        out_shape=tuple(jax.ShapeDtypeStruct(a.shape, a.dtype) for a in results),
        in_specs=[vmem] * 4,
        out_specs=(hbm,) * 4,
        scratch_shapes=[dma((18,))],
    )(*(pltpu.with_memory_space_constraint(a, pltpu.VMEM) for a in results))


def solution(mesh):
    rows = P("dp", "graph", None)
    flat = P("dp", "graph")
    return jax.shard_map(
        local,
        mesh=mesh,
        in_specs=(rows, rows, flat, flat, rows, flat, flat, P(), P(), P()),
        out_specs=(rows, rows, P(), P()),
        check_vma=False,
    )
```
